256 devices in a mesh: clus: 32 (over x, z), pair: 8 (over y, core).
Axes of the slice: x: 4, y: 4, z: 8, core: 2. Of those that a mesh axis runs over, the one named last changes fastest.
Arguments:
- child_basis: float32 [256, 256, 256], P('clus'), as said below
- transfer: float32 [256, 256, 256], P('clus'), may hold values from -0.5 to 0.5
- child_parent: int32 [32, 8], P('clus'), may hold values from 0 to 1, never falling along the last dimension, each value on 1 to 6 neighbouring positions
- upper_weight: float32 [64, 256, 256], P('clus'), as said below
- child_pairs: int32 [3072, 2], P(('clus', 'pair')), may hold values from -1 to 255, as said below
- child_blocks: float32 [3072, 256, 256], P(('clus', 'pair')), may hold values from -0.15625 to 0.15625
- parent_pairs: int32 [2048, 2], P(('clus', 'pair')), may hold values from -1 to 63, as said below
- parent_blocks: float32 [2048, 256, 256], P(('clus', 'pair')), may hold values from -0.15625 to 0.15625
Outputs:
- child_weight: float32 [256, 256, 256], P('clus')
- parent_basis: float32 [64, 256, 256], P('clus')
The draws below stay inside these ranges and needn't reach their ends.
Inputs may be any that keep to these rules, and one draw needn't show every extreme that they name: `child_pairs`: each device's aligned block of 12 rows holds its valid pairs first and then rows of -1, -1; every block has one valid row or more and some block is full. In the block of flat device index d (clus index c = d // 8), box i lies among the 8 boxes of clus index c, box j among those of clus indices c to c + 3, and j differs from i. `parent_pairs`: as for child_pairs, with blocks of 8 rows and the 2 parent boxes of each clus index. `child_basis`: symmetric positive definite. `upper_weight`: symmetric positive definite.
All inputs are finite; a program needn't handle non-finite values.
Results may differ from the reference program's by a relative error of at most 0.0003.
Values sent between devices are 32-bit elements; how exact they have to be, the bound alone decides.
No kernel may reach another device: no remote copies, remote signals or barrier semaphores. Data moves between devices by JAX's collectives and lax.ppermute only.
A program may use at most 128 MiB of HBM per device.

```python
import math
import jax
import jax.numpy as jnp
import numpy as np
from jax import lax

RANK = 256
CHILD_DEV = 8
CPAIR_DEV = 12
PPAIR_DEV = 8
REACH = 3
MOST_KIDS = 6
PARENT_DEV = 2
NCHILD = 256
NPARENT = 64
NCPAIR = 3072
NPPAIR = 2048
N_CLUS = 32
N_PAIR = 8


def gram_draw(seed_key, box_total):
    subkeys = jax.random.split(seed_key, 2)
    diagonal = jnp.exp(jax.random.uniform(subkeys[0], (box_total, RANK), jnp.float32, math.log(2.5), math.log(6.0)))
    symmetric = jax.random.normal(subkeys[1], (box_total, RANK, RANK), jnp.float32)
    symmetric = (symmetric + jnp.swapaxes(symmetric, 1, 2)) / math.sqrt(2.0 * RANK)
    gram_set = symmetric + diagonal[:, :, None] * jnp.eye(RANK, dtype=jnp.float32)[None]
    return gram_set.astype(jnp.float32)


def pair_draw(seed_key, per_device, box_count):
    device_total = N_CLUS * N_PAIR
    total_rows = device_total * per_device
    row_ids = jnp.arange(total_rows, dtype=jnp.int32)
    device_ids = row_ids // per_device
    owner_ids = device_ids // N_PAIR
    slot_ids = row_ids % per_device
    subkeys = jax.random.split(seed_key, 5)
    near_local = jax.random.randint(subkeys[0], (total_rows,), 0, box_count, dtype=jnp.int32)
    reach_step = jax.random.randint(subkeys[1], (total_rows,), 0, REACH + 1, dtype=jnp.int32)
    far_owner = jnp.minimum(owner_ids + reach_step, N_CLUS - 1)
    far_local = jax.random.randint(subkeys[2], (total_rows,), 0, box_count, dtype=jnp.int32)
    marked = row_ids == total_rows - per_device
    near_local = jnp.where(marked, 0, near_local)
    far_local = jnp.where(marked, box_count - 1, far_local)
    far_owner = jnp.where(marked, N_CLUS - 1, far_owner)
    collide = (far_owner == owner_ids) & (far_local == near_local)
    far_local = jnp.where(collide, (near_local + 1) % box_count, far_local)
    counts = jax.random.randint(subkeys[3], (device_total,), per_device // 2, per_device, dtype=jnp.int32)
    chosen_device = jax.random.randint(subkeys[4], (), 0, device_total, dtype=jnp.int32)
    counts = jnp.where(jnp.arange(device_total, dtype=jnp.int32) == chosen_device, per_device, counts)
    usable = slot_ids < counts[device_ids]
    near_box = jnp.where(usable, owner_ids * box_count + near_local, -1)
    far_box = jnp.where(usable, far_owner * box_count + far_local, -1)
    return jnp.stack([near_box, far_box], axis=1).astype(jnp.int32)


def draw_child_basis(key, part):
    return gram_draw(jax.random.fold_in(key, 11), NCHILD)


def draw_upper_weight(key, part):
    return gram_draw(jax.random.fold_in(key, 12), NPARENT)


def draw_child_pairs(key, part):
    return pair_draw(jax.random.fold_in(key, 13), CPAIR_DEV, CHILD_DEV)


def draw_parent_pairs(key, part):
    return pair_draw(jax.random.fold_in(key, 14), PPAIR_DEV, PARENT_DEV)


def steps_of(key, shape, pieces, smallest, largest):
    def one(dim, blocks):
        draws = jax.random.uniform(jax.random.fold_in(jax.random.fold_in(key, 6), dim), (blocks,), jnp.float32, smallest / len(pieces), largest / len(pieces))
        return jnp.repeat(jnp.exp(draws), shape[dim] // blocks).reshape((-1,) + (1,) * (len(shape) - dim - 1))

    gain = one(*pieces[0])
    for cut in pieces[1:]:
        gain = gain * one(*cut)
    return gain


def length_profile(number_of, total, reach, slope):
    weights = [(1 << 20) // math.isqrt(grade ** slope) + 1 for grade in range(2, number_of + 1)]
    rest, given = total - reach - (number_of - 1), [1] * (number_of - 1)
    while rest > 0:
        free = [i for i in range(number_of - 1) if given[i] < reach]
        whole, remaining = sum([weights[i] for i in free]), rest
        for i in free:
            more = min(reach - given[i], max(1, remaining * weights[i] // whole), rest)
            given[i] = given[i] + more
            rest = rest - more
    return np.array([reach] + given)


def uneven_parts(rng, amount, total, reach, skew):
    if amount == 2:
        one = jax.random.randint(rng, (), max(1, total - reach), min(reach, total - 1) + 1)
        return jnp.stack([one, total - one])
    sizes = jnp.asarray(length_profile(amount, total, reach, skew), jnp.int32)
    twos = (amount - 1) // 2
    donor, taker = sizes[1:1 + 2 * twos:2], sizes[2:2 + 2 * twos:2]
    slack = jnp.minimum(donor - 1, reach - taker)
    passed = jax.random.randint(jax.random.fold_in(rng, 1), (twos,), 0, 1 << 20) % (slack + 1)
    sizes = sizes.at[1:1 + 2 * twos:2].set(donor - passed).at[2:2 + 2 * twos:2].set(taker + passed)
    return sizes[jax.random.permutation(jax.random.fold_in(rng, 2), amount)]


def normal_values(own_key, shape, width, limit, shards=(), kind=jnp.bfloat16):
    values = jax.random.normal(own_key, shape, jnp.float32) * width
    if len(shards) > 0:
        values = steps_of(own_key, shape, shards, -0.22, 0.18) * values
    return jnp.clip(values, min=-limit, max=limit).astype(kind)


def setup_inputs(seed: int = 0) -> dict:
    arg_keys = jax.random.split(jax.random.key(seed), 9)
    child_basis = draw_child_basis(jax.random.fold_in(arg_keys[8], 71), 0)
    transfer = normal_values(arg_keys[1], (NCHILD, RANK, RANK), (0.5 / RANK ** 0.5), 0.5, ((0, 32),), jnp.float32)
    child_parent = jax.vmap(lambda own: jnp.searchsorted(jnp.cumsum(uneven_parts(own, PARENT_DEV, CHILD_DEV, MOST_KIDS, 1)), jnp.arange(CHILD_DEV), side="right"))(jax.random.split(arg_keys[2], N_CLUS)).reshape((N_CLUS, CHILD_DEV)).astype(jnp.int32)
    upper_weight = draw_upper_weight(jax.random.fold_in(arg_keys[8], 71), 0)
    child_pairs = draw_child_pairs(jax.random.fold_in(arg_keys[8], 71), 0)
    child_blocks = normal_values(arg_keys[5], (NCPAIR, RANK, RANK), (1.0 / (6 * RANK ** 0.5)), 0.15625, ((0, 256),), jnp.float32)
    parent_pairs = draw_parent_pairs(jax.random.fold_in(arg_keys[8], 71), 0)
    parent_blocks = normal_values(arg_keys[7], (NPPAIR, RANK, RANK), (1.0 / (6 * RANK ** 0.5)), 0.15625, ((0, 256),), jnp.float32)
    return dict(child_basis=child_basis, transfer=transfer, child_parent=child_parent, upper_weight=upper_weight, child_pairs=child_pairs, child_blocks=child_blocks, parent_pairs=parent_pairs, parent_blocks=parent_blocks)


HIGHEST = lax.Precision.HIGHEST


def coupling(pair_list, blocks, gram_set, per_block):
    extent = gram_set.shape[-1]
    box_total = gram_set.shape[0]
    grouped = pair_list.reshape(-1, per_block, 2)
    stacked = blocks.reshape(-1, per_block, extent, extent)

    def advance(weight, element):
        group_pairs, group_blocks = element
        usable = group_pairs[:, 0] >= 0
        near_index = jnp.where(usable, group_pairs[:, 0], 0).astype(jnp.int32)
        far_index = jnp.where(usable, group_pairs[:, 1], 0).astype(jnp.int32)
        near_gram = gram_set[near_index]
        far_gram = gram_set[far_index]
        near_term = jnp.einsum("pab,pbc->pac", group_blocks, far_gram, precision=HIGHEST)
        near_term = jnp.einsum("pac,pdc->pad", near_term, group_blocks, precision=HIGHEST)
        far_term = jnp.einsum("pba,pbc->pac", group_blocks, near_gram, precision=HIGHEST)
        far_term = jnp.einsum("pac,pcd->pad", far_term, group_blocks, precision=HIGHEST)
        factor = usable.astype(gram_set.dtype)[:, None, None]
        weight = weight.at[near_index].add(near_term * factor)
        weight = weight.at[far_index].add(far_term * factor)
        return weight, None

    start = jnp.zeros((box_total, extent, extent), gram_set.dtype)
    weight, unused = lax.scan(advance, start, (grouped, stacked))
    return weight


def reference(child_basis, transfer, child_parent, upper_weight, child_pairs, child_blocks, parent_pairs, parent_blocks):
    extent = child_basis.shape[-1]
    parent_index = ((jnp.arange(NCHILD) // CHILD_DEV) * PARENT_DEV + child_parent.reshape(-1)).astype(jnp.int32)
    lifted = jnp.einsum("cba,cbd->cad", transfer, child_basis, precision=HIGHEST)
    lifted = jnp.einsum("cad,cde->cae", lifted, transfer, precision=HIGHEST)
    parent_basis = jnp.zeros((NPARENT, extent, extent), child_basis.dtype).at[parent_index].add(lifted)
    parent_weight = upper_weight + coupling(parent_pairs, parent_blocks, parent_basis, PPAIR_DEV)
    chosen = parent_weight[parent_index]
    lowered = jnp.einsum("cab,cbd->cad", transfer, chosen, precision=HIGHEST)
    lowered = jnp.einsum("cad,ced->cae", lowered, transfer, precision=HIGHEST)
    child_weight = coupling(child_pairs, child_blocks, child_basis, CPAIR_DEV) + lowered
    return child_weight, parent_basis
```

```python
import functools

import jax
import jax.numpy as jnp
from jax import lax
from jax.experimental import pallas as pl
from jax.experimental.pallas import tpu as pltpu
from jax.sharding import PartitionSpec as P

REACH = 3
PAIR = 8
HALF = 128
PART = 256
DIAG = 320
SHARE = 328
UNROLL = 4
VMEM_LIMIT = 44 * 2**20

NN = (((1,), (0,)), ((), ()))
NT = (((1,), (1,)), ((), ()))
TN = (((0,), (0,)), ((), ()))

VMEM = pl.BlockSpec(memory_space=pltpu.VMEM)
SMEM = pl.BlockSpec(memory_space=pltpu.SMEM)
ANY = pl.BlockSpec(memory_space=pl.ANY)


def split(value):
    high = value.astype(jnp.bfloat16)
    return high, (value - high.astype(jnp.float32)).astype(jnp.bfloat16)


def product(left, right, dims):
    def one(a, b):
        return lax.dot_general(a, b, dims, preferred_element_type=jnp.float32)

    return one(left[0], right[0]) + (one(left[0], right[1]) + one(left[1], right[0]))


def inner(block, gram):
    block = split(block)
    return product(block, split(product(split(gram), block, NN)), TN)


def outer(block, gram):
    block = split(block)
    return product(split(product(block, split(gram), NN)), block, NT)


def grids():
    rows = lax.broadcasted_iota(jnp.int32, (HALF, HALF), 0)
    cols = lax.broadcasted_iota(jnp.int32, (HALF, HALF), 1)
    return rows, cols


def packed(full):
    rows, cols = grids()
    first, last = full[:HALF, :HALF], full[HALF:, HALF:]
    diagonal = jnp.sum(jnp.where(rows == cols, first, 0.0), axis=0, keepdims=True)
    return full[HALF:, :HALF], jnp.where(rows > cols, first, last), diagonal


def packed_sum(half):
    rows, cols = grids()
    first, last = half[:HALF, :HALF], half[HALF:, HALF:]
    diagonal = jnp.sum(jnp.where(rows == cols, 2.0 * first, 0.0), axis=0, keepdims=True)
    lower = half[HALF:, :HALF] + half[:HALF, HALF:].T
    both = jnp.where(rows > cols, first, last) + jnp.where(rows < cols, first, last).T
    return lower, both, diagonal


def halved(lower, both, diagonal):
    rows, cols = grids()
    zero = jnp.zeros((HALF, HALF), jnp.float32)
    first = jnp.where(rows > cols, both, jnp.where(rows == cols, 0.5 * diagonal, 0.0))
    last = jnp.where(rows < cols, both, jnp.where(rows == cols, 0.5 * both, 0.0))
    return jnp.concatenate(
        [jnp.concatenate([first, zero], axis=1), jnp.concatenate([lower, last], axis=1)], axis=0
    )


def place_of(box, me):
    return ((box ^ me) & 1) * 4 + (((box >> 1) - (me >> 1)) & 3)


def box_at(place, me):
    return ((((place & 3) + (me >> 1)) & 3) << 1) | ((place >> 2) ^ (me & 1))


def lift_kernel(where, parents, basis, transfer, parent_basis, own, share, rows_of_parents):
    me = where[1]
    parent_basis[...] = jnp.zeros_like(parent_basis)

    def lift(group, carry):
        for step in range(UNROLL):
            child = group * UNROLL + step
            parent_basis[parents[0, child]] += inner(transfer[child], basis[child])
        return carry

    lax.fori_loop(0, basis.shape[0] // UNROLL, lift, 0)
    diagonals = []
    for parent in range(2):
        lower, both, diagonal = packed(parent_basis[parent])
        rows_of_parents[parent * 256 : parent * 256 + HALF] = lower
        rows_of_parents[parent * 256 + HALF : parent * 256 + 256] = both
        diagonals.append(diagonal)
    for place in range(PAIR):
        box = box_at(place, me)
        lower, both, diagonal = packed(basis[box])
        own[place, :HALF] = lower
        own[place, HALF:PART] = both
        own[place, PART:DIAG] = rows_of_parents[pl.ds(pl.multiple_of(box * 64, 64), 64)]
        own[place, DIAG:] = jnp.concatenate(
            [diagonal, *diagonals, jnp.zeros((SHARE - DIAG - 3, HALF), jnp.float32)], axis=0
        )
    share[...] = own[0]


def blocks_in(child_blocks, parent_blocks, held, sems):
    copies = []
    count = child_blocks.shape[0] // UNROLL
    for group in range(count + parent_blocks.shape[0] // UNROLL):
        source, at = (child_blocks, group) if group < count else (parent_blocks, group - count)
        copy = pltpu.make_async_copy(
            source.at[pl.ds(at * UNROLL, UNROLL)],
            held.at[pl.ds(group * UNROLL, UNROLL)],
            sems.at[group],
        )
        copy.start()
        copies.append(copy)
    return copies


def far_kernel(
    where, child_pairs, parent_pairs, child_basis, parent_basis, child_blocks, parent_blocks,
    kept, sent, own, held, total, sems, out_sem,
):
    clus, me = where[0], where[1]
    copies = blocks_in(child_blocks, parent_blocks, held, sems)
    total[...] = jnp.zeros_like(total)
    trash = 4 * PAIR
    child_count = child_blocks.shape[0]
    for group, copy in enumerate(copies):
        copy.wait()
        terms = []
        for step in range(UNROLL):
            row = group * UNROLL + step
            if row < child_count:
                near = child_pairs[row, 0]
                gram = child_basis[jnp.where(near >= 0, near - clus * PAIR, 0)]
            else:
                near = parent_pairs[row - child_count, 0]
                gram = parent_basis[jnp.where(near >= 0, near - clus * 2, 0)]
            terms.append(packed(inner(held[row], gram)))
        for step in range(UNROLL):
            row = group * UNROLL + step
            lower, both, diagonal = terms[step]
            if row < child_count:
                far = child_pairs[row, 1]
                slot = place_of(far & 7, me) * 4 + (far >> 3) - clus
                slot = jnp.where(far >= 0, slot, trash)
                total[slot, :HALF] += lower
                total[slot, HALF:PART] += both
                total[slot, DIAG : DIAG + 1] += diagonal
            else:
                far = parent_pairs[row - child_count, 1]
                usable = far >= 0
                offset, parent = (far >> 1) - clus, far & 1
                pieces = (lower[:64], lower[64:], both[:64], both[64:])
                for piece, rows in enumerate(pieces):
                    slot = place_of(parent * 4 + piece, me) * 4 + offset
                    total[jnp.where(usable, slot, trash), PART:DIAG] += rows
                slot = jnp.where(usable, place_of(0, me) * 4 + offset, trash)
                lines = lax.broadcasted_iota(jnp.int32, (8, HALF), 0)
                total[slot, DIAG:] += jnp.where(lines == parent + 1, diagonal, 0.0)
    outs = []
    for place in range(PAIR):
        target = kept if place < 4 else sent
        outs.append((total.at[pl.ds(place * 4 + 1, REACH)], target.at[place & 3]))
    for place in range(PAIR):
        outs.append((total.at[place * 4], own.at[place]))
    outs = [pltpu.make_async_copy(a, b, out_sem.at[i]) for i, (a, b) in enumerate(outs)]
    for copy in outs:
        copy.start()
    for copy in outs:
        copy.wait()


def near_kernel(
    where, child_pairs, parent_pairs, child_blocks, parent_blocks, own_terms, own_window, *rest
):
    pieces = rest[:PAIR]
    kept, sent, held, window, total, rows_of_parents, sems, in_sem = rest[PAIR:]
    clus, me = where[0], where[1]
    loads = [pltpu.make_async_copy(own_window, window.at[:, 0], in_sem.at[PAIR])]
    for place in range(PAIR):
        loads.append(
            pltpu.make_async_copy(
                pieces[place], window.at[place, pl.ds(1, REACH)], in_sem.at[place]
            )
        )
    for copy in loads:
        copy.start()
    copies = blocks_in(child_blocks, parent_blocks, held, sems)
    total[...] = jnp.zeros_like(total)
    for copy in loads:
        copy.wait()
    child_count = child_blocks.shape[0]
    for group, copy in enumerate(copies):
        copy.wait()
        terms = []
        for step in range(UNROLL):
            row = group * UNROLL + step
            if row < child_count:
                far = child_pairs[row, 1]
                usable = far >= 0
                place = place_of(far & 7, me)
                offset = jnp.where(usable, (far >> 3) - clus, 0)
                gram = halved(
                    window[place, offset, :HALF],
                    window[place, offset, HALF:PART],
                    window[place, offset, DIAG : DIAG + 1],
                )
            else:
                far = parent_pairs[row - child_count, 1]
                usable = far >= 0
                parent = far & 1
                offset = jnp.where(usable, (far >> 1) - clus, 0)
                rows = [
                    window[place_of(parent * 4 + piece, me), offset, PART:DIAG]
                    for piece in range(4)
                ]
                diagonals = window[0, offset, DIAG:]
                gram = halved(
                    jnp.concatenate(rows[:2], axis=0),
                    jnp.concatenate(rows[2:], axis=0),
                    jnp.where(parent == 0, diagonals[1:2], diagonals[2:3]),
                )
            terms.append(outer(held[row], gram))
        for step in range(UNROLL):
            row = group * UNROLL + step
            if row < child_count:
                near = child_pairs[row, 0]
                slot = jnp.where(near >= 0, near - clus * PAIR, PAIR + 2)
            else:
                near = parent_pairs[row - child_count, 0]
                slot = jnp.where(near >= 0, PAIR + near - clus * 2, PAIR + 2)
            total[slot] += terms[step]
    diagonals = []
    for parent in range(2):
        lower, both, diagonal = packed_sum(total[PAIR + parent])
        rows_of_parents[parent * 256 : parent * 256 + HALF] = lower
        rows_of_parents[parent * 256 + HALF : parent * 256 + 256] = both
        diagonals.append(diagonal)
    for place in range(PAIR):
        target = kept if place < 4 else sent
        box = box_at(place, me)
        lower, both, diagonal = packed_sum(total[box])
        at = place & 3
        target[at, :HALF] = own_terms[place, :HALF] + lower
        target[at, HALF:PART] = own_terms[place, HALF:PART] + both
        target[at, PART:DIAG] = (
            own_terms[place, PART:DIAG] + rows_of_parents[pl.ds(pl.multiple_of(box * 64, 64), 64)]
        )
        of_parents = [jnp.where(box == 0, line, 0.0) for line in diagonals]
        target[at, DIAG:] = own_terms[place, DIAG:] + jnp.concatenate(
            [diagonal, *of_parents, jnp.zeros((SHARE - DIAG - 3, HALF), jnp.float32)], axis=0
        )


def lower_kernel(where, parents, transfer, upper, *rest):
    pieces, weight, shares, coarse, sems = rest[:PAIR], *rest[PAIR:]
    me = where[1]
    copies = [
        pltpu.make_async_copy(pieces[place], shares.at[place], sems.at[place])
        for place in range(PAIR)
    ]
    for copy in copies:
        copy.start()
    for copy in copies:
        copy.wait()
    diagonals = shares[place_of(0, me), DIAG:]
    for parent in range(2):
        rows = [shares[place_of(parent * 4 + piece, me), PART:DIAG] for piece in range(4)]
        coarse[parent] = 0.5 * upper[parent] + halved(
            jnp.concatenate(rows[:2], axis=0),
            jnp.concatenate(rows[2:], axis=0),
            diagonals[parent + 1 : parent + 2],
        )

    def lower(group, carry):
        terms = []
        for step in range(UNROLL):
            child = group * UNROLL + step
            place = place_of(child, me)
            term = outer(transfer[child], coarse[parents[0, child]]) + halved(
                shares[place, :HALF], shares[place, HALF:PART], shares[place, DIAG : DIAG + 1]
            )
            weight[child] = term + term.T
        return carry

    lax.fori_loop(0, weight.shape[0] // UNROLL, lower, 0)


def call(kernel, name, out_shape, in_specs, out_specs, scratch, products):
    return pl.pallas_call(
        kernel,
        name=name,
        out_shape=out_shape,
        in_specs=in_specs,
        out_specs=out_specs,
        scratch_shapes=scratch,
        compiler_params=pltpu.CompilerParams(vmem_limit_bytes=VMEM_LIMIT),
        cost_estimate=pl.CostEstimate(
            flops=products * 6 * 256**3, bytes_accessed=8 * 2**20, transcendentals=0
        ),
    )


def floats(*shape):
    return jax.ShapeDtypeStruct(shape, jnp.float32)


def to_clus(value, steps):
    count = lax.axis_size("clus")
    return lax.ppermute(value, "clus", [(i, (i + steps) % count) for i in range(count)])


def to_y(value, steps):
    return lax.ppermute(value, "pair", [(i, (i + 2 * steps) % PAIR) for i in range(PAIR)])


def to_core(value):
    return lax.ppermute(value, "pair", [(i, i ^ 1) for i in range(PAIR)])


def per_device(
    child_basis,
    transfer,
    child_parent,
    upper_weight,
    child_pairs,
    child_blocks,
    parent_pairs,
    parent_blocks,
):
    boxes, extent = child_basis.shape[0], child_basis.shape[-1]
    pair_rows = child_blocks.shape[0] + parent_blocks.shape[0]
    groups = pair_rows // UNROLL
    where = jnp.stack([lax.axis_index("clus"), lax.axis_index("pair")]).astype(jnp.int32)

    parent_basis, own_window, share = call(
        lift_kernel,
        "lift",
        (floats(2, extent, extent), floats(PAIR, SHARE, HALF), floats(SHARE, HALF)),
        [SMEM, SMEM, VMEM, VMEM],
        (VMEM, VMEM, VMEM),
        [pltpu.VMEM((512, HALF), jnp.float32)],
        16,
    )(where, child_parent, child_basis, transfer)

    reached = jnp.stack([to_clus(share, -offset) for offset in range(1, REACH + 1)])

    kept, sent, own_terms = call(
        far_kernel,
        "far",
        (
            floats(4, REACH, SHARE, HALF),
            floats(4, REACH, SHARE, HALF),
            floats(PAIR, SHARE, HALF),
        ),
        [SMEM, SMEM, SMEM, VMEM, VMEM, ANY, ANY],
        (ANY, ANY, ANY),
        [
            pltpu.VMEM((pair_rows, extent, extent), jnp.float32),
            pltpu.VMEM((4 * PAIR + 1, SHARE, HALF), jnp.float32),
            pltpu.SemaphoreType.DMA((groups,)),
            pltpu.SemaphoreType.DMA((2 * PAIR,)),
        ],
        40,
    )(where, child_pairs, parent_pairs, child_basis, parent_basis, child_blocks, parent_blocks)

    window = [reached] + [to_y(reached, -step) for step in range(1, 4)]
    window = window + [to_core(piece) for piece in window]

    got = to_core(sent)
    parts = [kept[step] + got[step] for step in range(4)]
    far_sum = parts[0]
    for step in range(1, 4):
        far_sum = far_sum + to_y(parts[step], step)
    far_parts = [to_clus(far_sum[offset - 1], offset) for offset in range(1, REACH + 1)]

    kept, sent = call(
        near_kernel,
        "near",
        (floats(4, SHARE, HALF), floats(4, SHARE, HALF)),
        [SMEM, SMEM, SMEM, ANY, ANY, VMEM] + [ANY] * (PAIR + 1),
        (VMEM, VMEM),
        [
            pltpu.VMEM((pair_rows, extent, extent), jnp.float32),
            pltpu.VMEM((PAIR, REACH + 1, SHARE, HALF), jnp.float32),
            pltpu.VMEM((PAIR + 3, extent, extent), jnp.float32),
            pltpu.VMEM((512, HALF), jnp.float32),
            pltpu.SemaphoreType.DMA((groups,)),
            pltpu.SemaphoreType.DMA((PAIR + 1,)),
        ],
        40,
    )(
        where, child_pairs, parent_pairs, child_blocks, parent_blocks, own_terms, own_window,
        *window,
    )

    got = to_core(sent)
    parts = [kept[step] + got[step] for step in range(4)]
    total = parts[0] + far_parts[0] + far_parts[1] + far_parts[2]
    for step in range(1, 4):
        total = total + to_y(parts[step], step)

    whole = [total] + [to_y(total, -step) for step in range(1, 4)]
    whole = whole + [to_core(piece) for piece in whole]
    child_weight = call(
        lower_kernel,
        "lower",
        floats(boxes, extent, extent),
        [SMEM, SMEM, VMEM, VMEM] + [ANY] * PAIR,
        VMEM,
        [
            pltpu.VMEM((PAIR, SHARE, HALF), jnp.float32),
            pltpu.VMEM((2, extent, extent), jnp.float32),
            pltpu.SemaphoreType.DMA((PAIR,)),
        ],
        16,
    )(where, child_parent, transfer, upper_weight, *whole)
    return child_weight, parent_basis


def solution(mesh):
    return jax.shard_map(
        per_device,
        mesh=mesh,
        in_specs=(
            P("clus", None, None),
            P("clus", None, None),
            P("clus", None),
            P("clus", None, None),
            P(("clus", "pair"), None),
            P(("clus", "pair"), None, None),
            P(("clus", "pair"), None),
            P(("clus", "pair"), None, None),
        ),
        out_specs=(P("clus", None, None), P("clus", None, None)),
        check_vma=False,
    )
```

```python
import functools

import jax
import jax.numpy as jnp
from jax import lax
from jax.experimental import pallas as pl
from jax.experimental.pallas import tpu as pltpu
from jax.sharding import PartitionSpec as P

REACH = 3
PAIR = 8
HALF = 128
PART = 256
DIAG = 320
SHARE = 328
UNROLL = 4
PARENTS = 2
CHILD_LIST = 10
PARENT_LIST = 34
VMEM_LIMIT = 56 * 2**20

NN = (((1,), (0,)), ((), ()))
NT = (((1,), (1,)), ((), ()))
TN = (((0,), (0,)), ((), ()))

VMEM = pl.BlockSpec(memory_space=pltpu.VMEM)
SMEM = pl.BlockSpec(memory_space=pltpu.SMEM)
ANY = pl.BlockSpec(memory_space=pl.ANY)


def split(value):
    high = value.astype(jnp.bfloat16)
    return high, (value - high.astype(jnp.float32)).astype(jnp.bfloat16)


def product(left, right, dims):
    def one(a, b):
        return lax.dot_general(a, b, dims, preferred_element_type=jnp.float32)

    return one(left[0], right[0]) + (one(left[0], right[1]) + one(left[1], right[0]))


def inner(block, gram):
    block = split(block)
    return product(block, split(product(split(gram), block, NN)), TN)


def outer(block, gram):
    block = split(block)
    return product(split(product(block, split(gram), NN)), block, NT)


def grids():
    rows = lax.broadcasted_iota(jnp.int32, (HALF, HALF), 0)
    cols = lax.broadcasted_iota(jnp.int32, (HALF, HALF), 1)
    return rows, cols


def packed(full):
    rows, cols = grids()
    first, last = full[:HALF, :HALF], full[HALF:, HALF:]
    diagonal = jnp.sum(jnp.where(rows == cols, first, 0.0), axis=0, keepdims=True)
    return full[HALF:, :HALF], jnp.where(rows > cols, first, last), diagonal


def packed_sum(half):
    rows, cols = grids()
    first, last = half[:HALF, :HALF], half[HALF:, HALF:]
    diagonal = jnp.sum(jnp.where(rows == cols, 2.0 * first, 0.0), axis=0, keepdims=True)
    lower = half[HALF:, :HALF] + half[:HALF, HALF:].T
    both = jnp.where(rows > cols, first, last) + jnp.where(rows < cols, first, last).T
    return lower, both, diagonal


def halved(lower, both, diagonal):
    rows, cols = grids()
    zero = jnp.zeros((HALF, HALF), jnp.float32)
    first = jnp.where(rows > cols, both, jnp.where(rows == cols, 0.5 * diagonal, 0.0))
    last = jnp.where(rows < cols, both, jnp.where(rows == cols, 0.5 * both, 0.0))
    return jnp.concatenate(
        [jnp.concatenate([first, zero], axis=1), jnp.concatenate([lower, last], axis=1)], axis=0
    )


def place_of(box, me):
    return ((box ^ me) & 1) * 4 + (((box >> 1) - (me >> 1)) & 3)


def box_at(place, me):
    return ((((place & 3) + (me >> 1)) & 3) << 1) | ((place >> 2) ^ (me & 1))


def lift_kernel(
    where, basis_in, transfer_in, parent_basis, own_same, own_other, share,
    basis, transfer, rows_of_parents, sems,
):
    me = where[1]
    copies = []
    for group in range(basis.shape[0] // 2):
        at = pl.ds(group * 2, 2)
        for source, target, half in ((basis_in, basis, 0), (transfer_in, transfer, 1)):
            copy = pltpu.make_async_copy(source.at[at], target.at[at], sems.at[group * 2 + half])
            copy.start()
            copies.append(copy)
    parent_basis[...] = jnp.zeros_like(parent_basis)
    for group in range(0, basis.shape[0], UNROLL):
        for copy in copies[group : group + UNROLL]:
            copy.wait()
        terms = [
            (where[PARENTS + child], inner(transfer[child], basis[child]))
            for child in range(group, group + UNROLL)
        ]
        for parent, term in terms:
            parent_basis[parent] += term
    diagonals = []
    for parent in range(2):
        lower, both, diagonal = packed(parent_basis[parent])
        rows_of_parents[parent * 256 : parent * 256 + HALF] = lower
        rows_of_parents[parent * 256 + HALF : parent * 256 + 256] = both
        diagonals.append(diagonal)
    for place in range(PAIR):
        box = box_at(place, me)
        lower, both, diagonal = packed(basis[box])
        own, at = (own_same if place < 4 else own_other), place & 3
        own[at, :HALF] = lower
        own[at, HALF:PART] = both
        own[at, PART:DIAG] = rows_of_parents[pl.ds(pl.multiple_of(box * 64, 64), 64)]
        own[at, DIAG:] = jnp.concatenate(
            [diagonal, *diagonals, jnp.zeros((SHARE - DIAG - 3, HALF), jnp.float32)], axis=0
        )
    share[...] = own_same[0]


def blocks_in(child_blocks, parent_blocks, held, sems):
    copies = []
    count = child_blocks.shape[0] // UNROLL
    for group in range(count + parent_blocks.shape[0] // UNROLL):
        source, at = (child_blocks, group) if group < count else (parent_blocks, group - count)
        copy = pltpu.make_async_copy(
            source.at[pl.ds(at * UNROLL, UNROLL)],
            held.at[pl.ds(group * UNROLL, UNROLL)],
            sems.at[group],
        )
        copy.start()
        copies.append(copy)
    return copies


def far_kernel(
    where, basis_in, parent_in, child_blocks, parent_blocks, kept, sent, own,
    child_basis, parent_basis, held, total, sems, in_sem, out_sem,
):
    clus, me = where[0], where[1]
    loads = [
        pltpu.make_async_copy(basis_in, child_basis, in_sem.at[0]),
        pltpu.make_async_copy(parent_in, parent_basis, in_sem.at[1]),
    ]
    for copy in loads:
        copy.start()
    copies = blocks_in(child_blocks, parent_blocks, held, sems)
    total[...] = jnp.zeros_like(total)
    for copy in loads:
        copy.wait()
    trash = 4 * PAIR
    child_count = child_blocks.shape[0]
    for group, copy in enumerate(copies):
        copy.wait()
        terms = []
        for step in range(UNROLL):
            row = group * UNROLL + step
            if row < child_count:
                near = where[CHILD_LIST + 2 * row]
                gram = child_basis[jnp.where(near >= 0, near - clus * PAIR, 0)]
            else:
                near = where[PARENT_LIST + 2 * (row - child_count)]
                gram = parent_basis[jnp.where(near >= 0, near - clus * 2, 0)]
            terms.append(packed(inner(held[row], gram)))
        for step in range(UNROLL):
            row = group * UNROLL + step
            lower, both, diagonal = terms[step]
            if row < child_count:
                far = where[CHILD_LIST + 2 * row + 1]
                slot = place_of(far & 7, me) * 4 + (far >> 3) - clus
                slot = jnp.where(far >= 0, slot, trash)
                total[slot, :HALF] += lower
                total[slot, HALF:PART] += both
                total[slot, DIAG : DIAG + 1] += diagonal
            else:
                far = where[PARENT_LIST + 2 * (row - child_count) + 1]
                usable = far >= 0
                offset, parent = (far >> 1) - clus, far & 1
                pieces = (lower[:64], lower[64:], both[:64], both[64:])
                for piece, rows in enumerate(pieces):
                    slot = place_of(parent * 4 + piece, me) * 4 + offset
                    total[jnp.where(usable, slot, trash), PART:DIAG] += rows
                slot = jnp.where(usable, place_of(0, me) * 4 + offset, trash)
                lines = lax.broadcasted_iota(jnp.int32, (8, HALF), 0)
                total[slot, DIAG:] += jnp.where(lines == parent + 1, diagonal, 0.0)
    outs = []
    for place in range(PAIR):
        target = kept if place < 4 else sent
        outs.append((total.at[pl.ds(place * 4 + 1, REACH)], target.at[place & 3]))
    for place in range(PAIR):
        outs.append((total.at[place * 4], own.at[place]))
    outs = [pltpu.make_async_copy(a, b, out_sem.at[i]) for i, (a, b) in enumerate(outs)]
    for copy in outs:
        copy.start()
    for copy in outs:
        copy.wait()


def near_kernel(
    where, after, also_after, child_blocks, parent_blocks, own_terms, own_same, own_other, first, other_first,
    *rest,
):
    pieces = rest[: 2 * PAIR]
    kept, sent, held, window, total, rows_of_parents, sems, in_sem = rest[2 * PAIR :]
    clus, me = where[0], where[1]
    halves = ((own_same, 0, 0), (own_other, 4, 0), (first, 0, 1), (other_first, 4, 1))
    loads = [
        pltpu.make_async_copy(source, window.at[pl.ds(at, 4), offset], in_sem.at[i])
        for i, (source, at, offset) in enumerate(halves)
    ]
    for i, piece in enumerate(pieces):
        loads.append(
            pltpu.make_async_copy(piece, window.at[i % PAIR, 2 + i // PAIR], in_sem.at[4 + i])
        )
    for copy in loads:
        copy.start()
    copies = blocks_in(child_blocks, parent_blocks, held, sems)
    total[...] = jnp.zeros_like(total)
    for copy in loads:
        copy.wait()
    child_count = child_blocks.shape[0]
    for group, copy in enumerate(copies):
        copy.wait()
        terms = []
        for step in range(UNROLL):
            row = group * UNROLL + step
            if row < child_count:
                far = where[CHILD_LIST + 2 * row + 1]
                usable = far >= 0
                place = place_of(far & 7, me)
                offset = jnp.where(usable, (far >> 3) - clus, 0)
                gram = halved(
                    window[place, offset, :HALF],
                    window[place, offset, HALF:PART],
                    window[place, offset, DIAG : DIAG + 1],
                )
            else:
                far = where[PARENT_LIST + 2 * (row - child_count) + 1]
                usable = far >= 0
                parent = far & 1
                offset = jnp.where(usable, (far >> 1) - clus, 0)
                rows = [
                    window[place_of(parent * 4 + piece, me), offset, PART:DIAG]
                    for piece in range(4)
                ]
                diagonals = window[0, offset, DIAG:]
                gram = halved(
                    jnp.concatenate(rows[:2], axis=0),
                    jnp.concatenate(rows[2:], axis=0),
                    jnp.where(parent == 0, diagonals[1:2], diagonals[2:3]),
                )
            terms.append(outer(held[row], gram))
        for step in range(UNROLL):
            row = group * UNROLL + step
            if row < child_count:
                near = where[CHILD_LIST + 2 * row]
                slot = jnp.where(near >= 0, near - clus * PAIR, PAIR + 2)
            else:
                near = where[PARENT_LIST + 2 * (row - child_count)]
                slot = jnp.where(near >= 0, PAIR + near - clus * 2, PAIR + 2)
            total[slot] += terms[step]
    diagonals = []
    for parent in range(2):
        lower, both, diagonal = packed_sum(total[PAIR + parent])
        rows_of_parents[parent * 256 : parent * 256 + HALF] = lower
        rows_of_parents[parent * 256 + HALF : parent * 256 + 256] = both
        diagonals.append(diagonal)
    for place in range(PAIR):
        target = kept if place < 4 else sent
        box = box_at(place, me)
        lower, both, diagonal = packed_sum(total[box])
        at = place & 3
        target[at, :HALF] = own_terms[place, :HALF] + lower
        target[at, HALF:PART] = own_terms[place, HALF:PART] + both
        target[at, PART:DIAG] = (
            own_terms[place, PART:DIAG] + rows_of_parents[pl.ds(pl.multiple_of(box * 64, 64), 64)]
        )
        of_parents = [jnp.where(box == 0, line, 0.0) for line in diagonals]
        target[at, DIAG:] = own_terms[place, DIAG:] + jnp.concatenate(
            [diagonal, *of_parents, jnp.zeros((SHARE - DIAG - 3, HALF), jnp.float32)], axis=0
        )


def lower_kernel(where, transfer, upper, *rest):
    pieces, weight, shares, coarse, sems = rest[:PAIR], *rest[PAIR:]
    me = where[1]
    copies = [
        pltpu.make_async_copy(pieces[place], shares.at[place], sems.at[place])
        for place in range(PAIR)
    ]
    for copy in copies:
        copy.start()
    for copy in copies:
        copy.wait()
    diagonals = shares[place_of(0, me), DIAG:]
    for parent in range(2):
        rows = [shares[place_of(parent * 4 + piece, me), PART:DIAG] for piece in range(4)]
        coarse[parent] = 0.5 * upper[parent] + halved(
            jnp.concatenate(rows[:2], axis=0),
            jnp.concatenate(rows[2:], axis=0),
            diagonals[parent + 1 : parent + 2],
        )

    def lower(group, carry):
        terms = []
        for step in range(UNROLL):
            child = group * UNROLL + step
            place = place_of(child, me)
            term = outer(transfer[child], coarse[where[PARENTS + child]]) + halved(
                shares[place, :HALF], shares[place, HALF:PART], shares[place, DIAG : DIAG + 1]
            )
            weight[child] = term + term.T
        return carry

    lax.fori_loop(0, weight.shape[0] // UNROLL, lower, 0)


def call(kernel, name, out_shape, in_specs, out_specs, scratch, products):
    return pl.pallas_call(
        kernel,
        name=name,
        out_shape=out_shape,
        in_specs=in_specs,
        out_specs=out_specs,
        scratch_shapes=scratch,
        compiler_params=pltpu.CompilerParams(vmem_limit_bytes=VMEM_LIMIT),
        cost_estimate=pl.CostEstimate(
            flops=products * 6 * 256**3, bytes_accessed=8 * 2**20, transcendentals=0
        ),
    )


def floats(*shape):
    return jax.ShapeDtypeStruct(shape, jnp.float32)


def to_clus(value, steps):
    count = lax.axis_size("clus")
    return lax.ppermute(value, "clus", [(i, (i + steps) % count) for i in range(count)])


def to_y(value, steps):
    return lax.ppermute(value, "pair", [(i, (i + 2 * steps) % PAIR) for i in range(PAIR)])


def to_core(value):
    return lax.ppermute(value, "pair", [(i, i ^ 1) for i in range(PAIR)])


def everywhere(share):
    pieces = [share] + [to_y(share, -step) for step in range(1, 4)]
    return pieces + [to_core(piece) for piece in pieces]


def per_device(
    child_basis,
    transfer,
    child_parent,
    upper_weight,
    child_pairs,
    child_blocks,
    parent_pairs,
    parent_blocks,
):
    boxes, extent = child_basis.shape[0], child_basis.shape[-1]
    pair_rows = child_blocks.shape[0] + parent_blocks.shape[0]
    groups = pair_rows // UNROLL
    where = jnp.concatenate(
        [
            jnp.stack([lax.axis_index("clus"), lax.axis_index("pair")]).astype(jnp.int32),
            child_parent.reshape(-1),
            child_pairs.reshape(-1),
            parent_pairs.reshape(-1),
        ]
    )

    parent_basis, own_same, own_other, share = call(
        lift_kernel,
        "lift",
        (
            floats(2, extent, extent),
            floats(4, SHARE, HALF),
            floats(4, SHARE, HALF),
            floats(SHARE, HALF),
        ),
        [SMEM, ANY, ANY],
        (VMEM, VMEM, VMEM, VMEM),
        [
            pltpu.VMEM((boxes, extent, extent), jnp.float32),
            pltpu.VMEM((boxes, extent, extent), jnp.float32),
            pltpu.VMEM((512, HALF), jnp.float32),
            pltpu.SemaphoreType.DMA((boxes,)),
        ],
        16,
    )(where, child_basis, transfer)

    second = to_clus(share, -2)

    kept, sent, own_terms = call(
        far_kernel,
        "far",
        (
            floats(4, REACH, SHARE, HALF),
            floats(4, REACH, SHARE, HALF),
            floats(PAIR, SHARE, HALF),
        ),
        [SMEM, ANY, ANY, ANY, ANY],
        (ANY, ANY, ANY),
        [
            pltpu.VMEM((boxes, extent, extent), jnp.float32),
            pltpu.VMEM((2, extent, extent), jnp.float32),
            pltpu.VMEM((pair_rows, extent, extent), jnp.float32),
            pltpu.VMEM((4 * PAIR + 1, SHARE, HALF), jnp.float32),
            pltpu.SemaphoreType.DMA((groups,)),
            pltpu.SemaphoreType.DMA((2,)),
            pltpu.SemaphoreType.DMA((2 * PAIR,)),
        ],
        40,
    )(where, child_basis, parent_basis, child_blocks, parent_blocks)

    second, own_same, kept, sent = lax.optimization_barrier((second, own_same, kept, sent))
    barrier = lax.optimization_barrier
    third = to_clus(second, -1)
    got = to_core(sent)
    seconds = [second] + [to_y(second, -step) for step in range(1, 4)]
    third, got, seconds = barrier((third, got, seconds))

    first = to_clus(own_same, -1)
    far_first = to_clus(kept[:, 0] + got[:, 0], 1)
    parts = [kept[step, 1:] + got[step, 1:] for step in range(4)]
    received = [to_y(parts[step], step) for step in range(1, 4)]
    first, far_first, received, third, seconds = barrier(
        (first, far_first, received, third, seconds)
    )

    far_sum = parts[0] + received[0] + received[1] + received[2]
    far_third = to_clus(far_sum[1], 1)
    thirds = [third] + [to_y(third, -step) for step in range(1, 4)]
    far_third, thirds, first, seconds = barrier((far_third, thirds, first, seconds))

    far_later = to_clus(far_sum[0] + far_third, 2)
    other_first = to_core(first)
    second_pieces = seconds + [to_core(piece) for piece in seconds]
    third_pieces = thirds + [to_core(piece) for piece in thirds]

    kept, sent = call(
        near_kernel,
        "near",
        (floats(4, SHARE, HALF), floats(4, SHARE, HALF)),
        [SMEM, ANY, ANY, ANY, ANY, VMEM] + [ANY] * (2 * PAIR + 4),
        (VMEM, VMEM),
        [
            pltpu.VMEM((pair_rows, extent, extent), jnp.float32),
            pltpu.VMEM((PAIR, REACH + 1, SHARE, HALF), jnp.float32),
            pltpu.VMEM((PAIR + 3, extent, extent), jnp.float32),
            pltpu.VMEM((512, HALF), jnp.float32),
            pltpu.SemaphoreType.DMA((groups,)),
            pltpu.SemaphoreType.DMA((2 * PAIR + 4,)),
        ],
        40,
    )(
        where, far_third, far_first, child_blocks, parent_blocks, own_terms, own_same, own_other,
        first, other_first, *second_pieces, *third_pieces,
    )

    kept, sent, far_later = lax.optimization_barrier((kept, sent, far_later))
    got = to_core(sent)
    parts = [kept[step] + got[step] + far_first[step] for step in range(4)]
    total = parts[0] + far_later
    for step in range(1, 4):
        total = total + to_y(parts[step], step)

    child_weight = call(
        lower_kernel,
        "lower",
        floats(boxes, extent, extent),
        [SMEM, VMEM, VMEM] + [ANY] * PAIR,
        VMEM,
        [
            pltpu.VMEM((PAIR, SHARE, HALF), jnp.float32),
            pltpu.VMEM((2, extent, extent), jnp.float32),
            pltpu.SemaphoreType.DMA((PAIR,)),
        ],
        16,
    )(where, transfer, upper_weight, *everywhere(total))
    return child_weight, parent_basis


def solution(mesh):
    return jax.shard_map(
        per_device,
        mesh=mesh,
        in_specs=(
            P("clus", None, None),
            P("clus", None, None),
            P("clus", None),
            P("clus", None, None),
            P(("clus", "pair"), None),
            P(("clus", "pair"), None, None),
            P(("clus", "pair"), None),
            P(("clus", "pair"), None, None),
        ),
        out_specs=(P("clus", None, None), P("clus", None, None)),
        check_vma=False,
    )
```

```python
import functools

import jax
import jax.numpy as jnp
from jax import lax
from jax.experimental import pallas as pl
from jax.experimental.pallas import tpu as pltpu
from jax.sharding import PartitionSpec as P

REACH = 3
PAIR = 8
HALF = 128
PART = 256
DIAG = 320
SHARE = 328
UNROLL = 4
PARENTS = 2
CHILD_LIST = 10
PARENT_LIST = 34
VMEM_LIMIT = 24 * 2**20

NN = (((1,), (0,)), ((), ()))
NT = (((1,), (1,)), ((), ()))
TN = (((0,), (0,)), ((), ()))

VMEM = pl.BlockSpec(memory_space=pltpu.VMEM)
SMEM = pl.BlockSpec(memory_space=pltpu.SMEM)
ANY = pl.BlockSpec(memory_space=pl.ANY)


def split(value):
    high = value.astype(jnp.bfloat16)
    return high, (value - high.astype(jnp.float32)).astype(jnp.bfloat16)


def product(left, right, dims):
    def one(a, b):
        return lax.dot_general(a, b, dims, preferred_element_type=jnp.float32)

    return one(left[0], right[0]) + (one(left[0], right[1]) + one(left[1], right[0]))


def inner(blocks, grams):
    blocks = [split(block) for block in blocks]
    grams = [split(gram) for gram in grams]
    halfway = [split(product(gram, block, NN)) for gram, block in zip(grams, blocks)]
    return [product(block, value, TN) for block, value in zip(blocks, halfway)]


def outer(blocks, grams):
    blocks = [split(block) for block in blocks]
    grams = [split(gram) for gram in grams]
    halfway = [split(product(block, gram, NN)) for gram, block in zip(grams, blocks)]
    return [product(value, block, NT) for block, value in zip(blocks, halfway)]


def each(count, body):
    lax.fori_loop(0, count, lambda i, carry: (body(i), carry)[1], 0)


def cleared(ref):
    def clear(i):
        ref[i] = jnp.zeros(ref.shape[1:], ref.dtype)

    each(ref.shape[0], clear)


def grids():
    rows = lax.broadcasted_iota(jnp.int32, (HALF, HALF), 0)
    cols = lax.broadcasted_iota(jnp.int32, (HALF, HALF), 1)
    return rows, cols


def packed(full):
    rows, cols = grids()
    first, last = full[:HALF, :HALF], full[HALF:, HALF:]
    diagonal = jnp.sum(jnp.where(rows == cols, first, 0.0), axis=0, keepdims=True)
    return full[HALF:, :HALF], jnp.where(rows > cols, first, last), diagonal


def packed_sum(half):
    rows, cols = grids()
    first, last = half[:HALF, :HALF], half[HALF:, HALF:]
    diagonal = jnp.sum(jnp.where(rows == cols, 2.0 * first, 0.0), axis=0, keepdims=True)
    lower = half[HALF:, :HALF] + half[:HALF, HALF:].T
    both = jnp.where(rows > cols, first, last) + jnp.where(rows < cols, first, last).T
    return lower, both, diagonal


def halved(lower, both, diagonal):
    rows, cols = grids()
    zero = jnp.zeros((HALF, HALF), jnp.float32)
    first = jnp.where(rows > cols, both, jnp.where(rows == cols, 0.5 * diagonal, 0.0))
    last = jnp.where(rows < cols, both, jnp.where(rows == cols, 0.5 * both, 0.0))
    return jnp.concatenate(
        [jnp.concatenate([first, zero], axis=1), jnp.concatenate([lower, last], axis=1)], axis=0
    )


def place_of(box, me):
    return ((box ^ me) & 1) * 4 + (((box >> 1) - (me >> 1)) & 3)


def box_at(place, me):
    return ((((place & 3) + (me >> 1)) & 3) << 1) | ((place >> 2) ^ (me & 1))


def lift_kernel(
    where, basis_in, transfer_in, parent_basis, own_same, own_other, share,
    basis, transfer, rows_of_parents, sems,
):
    me = where[1]
    count = basis.shape[0] // UNROLL

    def copies(group):
        at = pl.ds(group * UNROLL, UNROLL)
        return [
            pltpu.make_async_copy(basis_in.at[at], basis.at[at], sems.at[0, group]),
            pltpu.make_async_copy(transfer_in.at[at], transfer.at[at], sems.at[1, group]),
        ]

    for group in range(count):
        for copy in copies(group):
            copy.start()
    cleared(parent_basis)

    def lift(group):
        for copy in copies(group):
            copy.wait()
        children = [group * UNROLL + step for step in range(UNROLL)]
        terms = inner([transfer[c] for c in children], [basis[c] for c in children])
        for child, term in zip(children, terms):
            parent_basis[where[PARENTS + child]] += term

    each(count, lift)
    diagonals = []
    for parent in range(2):
        lower, both, diagonal = packed(parent_basis[parent])
        rows_of_parents[parent * 256 : parent * 256 + HALF] = lower
        rows_of_parents[parent * 256 + HALF : parent * 256 + 256] = both
        diagonals.append(diagonal)
    for own, first in ((own_same, 0), (own_other, 4)):

        def pack(at):
            box = box_at(first + at, me)
            lower, both, diagonal = packed(basis[box])
            own[at, :HALF] = lower
            own[at, HALF:PART] = both
            own[at, PART:DIAG] = rows_of_parents[pl.ds(pl.multiple_of(box * 64, 64), 64)]
            own[at, DIAG:] = jnp.concatenate(
                [diagonal, *diagonals, jnp.zeros((SHARE - DIAG - 3, HALF), jnp.float32)], axis=0
            )

        each(4, pack)
    share[...] = own_same[0]


def far_kernel(
    where, child_basis, parent_basis, child_blocks, parent_blocks, kept, sent, own, total,
):
    clus, me = where[0], where[1]
    child_groups = child_blocks.shape[0] // UNROLL
    parent_groups = parent_blocks.shape[0] // UNROLL
    cleared(total)
    trash = 4 * PAIR

    def of_children(group):
        rows = [group * UNROLL + step for step in range(UNROLL)]
        nears = [where[CHILD_LIST + 2 * row] for row in rows]
        grams = [child_basis[jnp.where(near >= 0, near - clus * PAIR, 0)] for near in nears]
        for row, term in zip(rows, inner([child_blocks[row] for row in rows], grams)):
            lower, both, diagonal = packed(term)
            far = where[CHILD_LIST + 2 * row + 1]
            slot = place_of(far & 7, me) * 4 + (far >> 3) - clus
            slot = jnp.where(far >= 0, slot, trash)
            total[slot, :HALF] += lower
            total[slot, HALF:PART] += both
            total[slot, DIAG : DIAG + 1] += diagonal

    def of_parents(group):
        rows = [group * UNROLL + step for step in range(UNROLL)]
        nears = [where[PARENT_LIST + 2 * row] for row in rows]
        grams = [parent_basis[jnp.where(near >= 0, near - clus * 2, 0)] for near in nears]
        blocks = [parent_blocks[row] for row in rows]
        for row, term in zip(rows, inner(blocks, grams)):
            lower, both, diagonal = packed(term)
            far = where[PARENT_LIST + 2 * row + 1]
            usable = far >= 0
            offset, parent = (far >> 1) - clus, far & 1
            pieces = (lower[:64], lower[64:], both[:64], both[64:])
            for piece, lines in enumerate(pieces):
                slot = place_of(parent * 4 + piece, me) * 4 + offset
                total[jnp.where(usable, slot, trash), PART:DIAG] += lines
            slot = jnp.where(usable, place_of(0, me) * 4 + offset, trash)
            lines = lax.broadcasted_iota(jnp.int32, (8, HALF), 0)
            total[slot, DIAG:] += jnp.where(lines == parent + 1, diagonal, 0.0)

    each(child_groups, of_children)
    each(parent_groups, of_parents)
    for target, first_place in ((kept, 0), (sent, 4)):

        def hand_out(at):
            place = first_place + at
            own[place] = total[place * 4]
            for offset in range(REACH):
                target[at, offset] = total[place * 4 + 1 + offset]

        each(4, hand_out)


def near_kernel(
    where, after, also_after, child_blocks, parent_blocks, own_terms, own_same, own_other, first, other_first,
    *rest,
):
    pieces = rest[: 2 * PAIR]
    kept, sent, window, total, rows_of_parents = rest[2 * PAIR :]
    clus, me = where[0], where[1]
    halves = ((own_same, 0, 0), (own_other, 4, 0), (first, 0, 1), (other_first, 4, 1))
    for source, first_place, offset in halves:

        def take_half(at):
            window[first_place + at, offset] = source[at]

        each(4, take_half)
    for i, piece in enumerate(pieces):
        window[i % PAIR, 2 + i // PAIR] = piece[...]
    child_groups = child_blocks.shape[0] // UNROLL
    parent_groups = parent_blocks.shape[0] // UNROLL
    cleared(total)
    trash = PAIR + 2

    def of_children(group):
        rows = [group * UNROLL + step for step in range(UNROLL)]
        grams = []
        for row in rows:
            far = where[CHILD_LIST + 2 * row + 1]
            place = place_of(far & 7, me)
            offset = jnp.where(far >= 0, (far >> 3) - clus, 0)
            grams.append(
                halved(
                    window[place, offset, :HALF],
                    window[place, offset, HALF:PART],
                    window[place, offset, DIAG : DIAG + 1],
                )
            )
        for row, term in zip(rows, outer([child_blocks[row] for row in rows], grams)):
            near = where[CHILD_LIST + 2 * row]
            total[jnp.where(near >= 0, near - clus * PAIR, trash)] += term

    def of_parents(group):
        rows = [group * UNROLL + step for step in range(UNROLL)]
        grams = []
        for row in rows:
            far = where[PARENT_LIST + 2 * row + 1]
            parent = far & 1
            offset = jnp.where(far >= 0, (far >> 1) - clus, 0)
            lines = [
                window[place_of(parent * 4 + piece, me), offset, PART:DIAG] for piece in range(4)
            ]
            diagonals = window[0, offset, DIAG:]
            grams.append(
                halved(
                    jnp.concatenate(lines[:2], axis=0),
                    jnp.concatenate(lines[2:], axis=0),
                    jnp.where(parent == 0, diagonals[1:2], diagonals[2:3]),
                )
            )
        blocks = [parent_blocks[row] for row in rows]
        for row, term in zip(rows, outer(blocks, grams)):
            near = where[PARENT_LIST + 2 * row]
            total[jnp.where(near >= 0, PAIR + near - clus * 2, trash)] += term

    each(child_groups, of_children)
    each(parent_groups, of_parents)
    diagonals = []
    for parent in range(2):
        lower, both, diagonal = packed_sum(total[PAIR + parent])
        rows_of_parents[parent * 256 : parent * 256 + HALF] = lower
        rows_of_parents[parent * 256 + HALF : parent * 256 + 256] = both
        diagonals.append(diagonal)
    for target, first_place in ((kept, 0), (sent, 4)):

        def pack(at):
            place = first_place + at
            box = box_at(place, me)
            lower, both, diagonal = packed_sum(total[box])
            target[at, :HALF] = own_terms[place, :HALF] + lower
            target[at, HALF:PART] = own_terms[place, HALF:PART] + both
            target[at, PART:DIAG] = (
                own_terms[place, PART:DIAG]
                + rows_of_parents[pl.ds(pl.multiple_of(box * 64, 64), 64)]
            )
            lines = [jnp.where(box == 0, line, 0.0) for line in diagonals]
            target[at, DIAG:] = own_terms[place, DIAG:] + jnp.concatenate(
                [diagonal, *lines, jnp.zeros((SHARE - DIAG - 3, HALF), jnp.float32)], axis=0
            )

        each(4, pack)


def lower_kernel(where, transfer, upper, *rest):
    pieces, weight, shares, coarse = rest[:PAIR], *rest[PAIR:]
    me = where[1]
    for place in range(PAIR):
        shares[place] = pieces[place][...]
    diagonals = shares[place_of(0, me), DIAG:]
    for parent in range(2):
        rows = [shares[place_of(parent * 4 + piece, me), PART:DIAG] for piece in range(4)]
        coarse[parent] = 0.5 * upper[parent] + halved(
            jnp.concatenate(rows[:2], axis=0),
            jnp.concatenate(rows[2:], axis=0),
            diagonals[parent + 1 : parent + 2],
        )

    def lower(group):
        children = [group * UNROLL + step for step in range(UNROLL)]
        terms = outer(
            [transfer[child] for child in children],
            [coarse[where[PARENTS + child]] for child in children],
        )
        for child, term in zip(children, terms):
            place = place_of(child, me)
            term = term + halved(
                shares[place, :HALF], shares[place, HALF:PART], shares[place, DIAG : DIAG + 1]
            )
            weight[child] = term + term.T

    each(weight.shape[0] // UNROLL, lower)


def call(kernel, name, out_shape, in_specs, out_specs, scratch, products):
    return pl.pallas_call(
        kernel,
        name=name,
        out_shape=out_shape,
        in_specs=in_specs,
        out_specs=out_specs,
        scratch_shapes=scratch,
        compiler_params=pltpu.CompilerParams(vmem_limit_bytes=VMEM_LIMIT),
        cost_estimate=pl.CostEstimate(
            flops=products * 6 * 256**3, bytes_accessed=8 * 2**20, transcendentals=0
        ),
    )


def floats(*shape):
    return jax.ShapeDtypeStruct(shape, jnp.float32)


def to_clus(value, steps):
    count = lax.axis_size("clus")
    return lax.ppermute(value, "clus", [(i, (i + steps) % count) for i in range(count)])


def to_y(value, steps):
    return lax.ppermute(value, "pair", [(i, (i + 2 * steps) % PAIR) for i in range(PAIR)])


def to_core(value):
    return lax.ppermute(value, "pair", [(i, i ^ 1) for i in range(PAIR)])


def everywhere(share):
    pieces = [share] + [to_y(share, -step) for step in range(1, 4)]
    return pieces + [to_core(piece) for piece in pieces]


def per_device(
    child_basis,
    transfer,
    child_parent,
    upper_weight,
    child_pairs,
    child_blocks,
    parent_pairs,
    parent_blocks,
):
    boxes, extent = child_basis.shape[0], child_basis.shape[-1]
    where = jnp.concatenate(
        [
            jnp.stack([lax.axis_index("clus"), lax.axis_index("pair")]).astype(jnp.int32),
            child_parent.reshape(-1),
            child_pairs.reshape(-1),
            parent_pairs.reshape(-1),
        ]
    )

    parent_basis, own_same, own_other, share = call(
        lift_kernel,
        "lift",
        (
            floats(2, extent, extent),
            floats(4, SHARE, HALF),
            floats(4, SHARE, HALF),
            floats(SHARE, HALF),
        ),
        [SMEM, ANY, ANY],
        (VMEM, VMEM, VMEM, VMEM),
        [
            pltpu.VMEM((boxes, extent, extent), jnp.float32),
            pltpu.VMEM((boxes, extent, extent), jnp.float32),
            pltpu.VMEM((512, HALF), jnp.float32),
            pltpu.SemaphoreType.DMA((2, boxes // UNROLL)),
        ],
        16,
    )(where, child_basis, transfer)

    second = to_clus(share, -2)

    kept, sent, own_terms = call(
        far_kernel,
        "far",
        (
            floats(4, REACH, SHARE, HALF),
            floats(4, REACH, SHARE, HALF),
            floats(PAIR, SHARE, HALF),
        ),
        [SMEM, VMEM, VMEM, VMEM, VMEM],
        (VMEM, VMEM, VMEM),
        [
            pltpu.VMEM((4 * PAIR + 1, SHARE, HALF), jnp.float32),
        ],
        40,
    )(where, child_basis, parent_basis, child_blocks, parent_blocks)

    second, own_same, kept, sent = lax.optimization_barrier((second, own_same, kept, sent))
    barrier = lax.optimization_barrier
    third = to_clus(second, -1)
    got = to_core(sent)
    seconds = [second] + [to_y(second, -step) for step in range(1, 4)]
    third, got, seconds = barrier((third, got, seconds))

    first = to_clus(own_same, -1)
    far_first = to_clus(kept[:, 0] + got[:, 0], 1)
    parts = [kept[step, 1:] + got[step, 1:] for step in range(4)]
    received = [to_y(parts[step], step) for step in range(1, 4)]
    first, far_first, received, third, seconds = barrier(
        (first, far_first, received, third, seconds)
    )

    far_sum = parts[0] + received[0] + received[1] + received[2]
    far_third = to_clus(far_sum[1], 1)
    thirds = [third] + [to_y(third, -step) for step in range(1, 4)]
    other_first = to_core(first)
    far_third, thirds, other_first, seconds = barrier((far_third, thirds, other_first, seconds))

    far_later = to_clus(far_sum[0] + far_third, 2)
    second_pieces = seconds + [to_core(piece) for piece in seconds]
    third_pieces = thirds + [to_core(piece) for piece in thirds]

    kept, sent = call(
        near_kernel,
        "near",
        (floats(4, SHARE, HALF), floats(4, SHARE, HALF)),
        [SMEM, ANY, ANY, VMEM, VMEM, VMEM] + [VMEM] * (2 * PAIR + 4),
        (VMEM, VMEM),
        [
            pltpu.VMEM((PAIR, REACH + 1, SHARE, HALF), jnp.float32),
            pltpu.VMEM((PAIR + 3, extent, extent), jnp.float32),
            pltpu.VMEM((512, HALF), jnp.float32),
        ],
        40,
    )(
        where, far_third, far_first, child_blocks, parent_blocks, own_terms, own_same, own_other,
        first, other_first, *second_pieces, *third_pieces,
    )

    kept, sent, far_later = lax.optimization_barrier((kept, sent, far_later))
    got = to_core(sent)
    parts = [kept[step] + got[step] + far_first[step] for step in range(4)]
    total = parts[0] + far_later
    for step in range(1, 4):
        total = total + to_y(parts[step], step)

    child_weight = call(
        lower_kernel,
        "lower",
        floats(boxes, extent, extent),
        [SMEM, VMEM, VMEM] + [VMEM] * PAIR,
        VMEM,
        [
            pltpu.VMEM((PAIR, SHARE, HALF), jnp.float32),
            pltpu.VMEM((2, extent, extent), jnp.float32),
        ],
        16,
    )(where, transfer, upper_weight, *everywhere(total))
    return child_weight, parent_basis


def solution(mesh):
    return jax.shard_map(
        per_device,
        mesh=mesh,
        in_specs=(
            P("clus", None, None),
            P("clus", None, None),
            P("clus", None),
            P("clus", None, None),
            P(("clus", "pair"), None),
            P(("clus", "pair"), None, None),
            P(("clus", "pair"), None),
            P(("clus", "pair"), None, None),
        ),
        out_specs=(P("clus", None, None), P("clus", None, None)),
        check_vma=False,
    )
```

```python
import functools

import jax
import jax.numpy as jnp
from jax import lax
from jax.experimental import pallas as pl
from jax.experimental.pallas import tpu as pltpu
from jax.sharding import PartitionSpec as P

REACH = 3
PAIR = 8
HALF = 128
PART = 256
DIAG = 320
SHARE = 328
UNROLL = 4
PARENTS = 2
CHILD_LIST = 10
PARENT_LIST = 34
VMEM_LIMIT = 24 * 2**20

NN = (((1,), (0,)), ((), ()))
NT = (((1,), (1,)), ((), ()))
TN = (((0,), (0,)), ((), ()))

VMEM = pl.BlockSpec(memory_space=pltpu.VMEM)
SMEM = pl.BlockSpec(memory_space=pltpu.SMEM)
ANY = pl.BlockSpec(memory_space=pl.ANY)


def split(value):
    high = value.astype(jnp.bfloat16)
    return high, (value - high.astype(jnp.float32)).astype(jnp.bfloat16)


def product(left, right, dims):
    def one(a, b):
        return lax.dot_general(a, b, dims, preferred_element_type=jnp.float32)

    return one(left[0], right[0]) + (one(left[0], right[1]) + one(left[1], right[0]))


def inner(blocks, grams):
    blocks = [split(block) for block in blocks]
    grams = [split(gram) for gram in grams]
    halfway = [split(product(gram, block, NN)) for gram, block in zip(grams, blocks)]
    return [product(block, value, TN) for block, value in zip(blocks, halfway)]


def outer(blocks, grams):
    blocks = [split(block) for block in blocks]
    grams = [split(gram) for gram in grams]
    halfway = [split(product(block, gram, NN)) for gram, block in zip(grams, blocks)]
    return [product(value, block, NT) for block, value in zip(blocks, halfway)]


def each(count, body):
    lax.fori_loop(0, count, lambda i, carry: (body(i), carry)[1], 0)


def cleared(ref):
    def clear(i):
        ref[i] = jnp.zeros(ref.shape[1:], ref.dtype)

    each(ref.shape[0], clear)


def grids():
    rows = lax.broadcasted_iota(jnp.int32, (HALF, HALF), 0)
    cols = lax.broadcasted_iota(jnp.int32, (HALF, HALF), 1)
    return rows, cols


def packed(full):
    rows, cols = grids()
    first, last = full[:HALF, :HALF], full[HALF:, HALF:]
    diagonal = jnp.sum(jnp.where(rows == cols, first, 0.0), axis=0, keepdims=True)
    return full[HALF:, :HALF], jnp.where(rows > cols, first, last), diagonal


def packed_sum(half):
    rows, cols = grids()
    first, last = half[:HALF, :HALF], half[HALF:, HALF:]
    diagonal = jnp.sum(jnp.where(rows == cols, 2.0 * first, 0.0), axis=0, keepdims=True)
    lower = half[HALF:, :HALF] + half[:HALF, HALF:].T
    both = jnp.where(rows > cols, first, last) + jnp.where(rows < cols, first, last).T
    return lower, both, diagonal


def halved(lower, both, diagonal):
    rows, cols = grids()
    zero = jnp.zeros((HALF, HALF), jnp.float32)
    first = jnp.where(rows > cols, both, jnp.where(rows == cols, 0.5 * diagonal, 0.0))
    last = jnp.where(rows < cols, both, jnp.where(rows == cols, 0.5 * both, 0.0))
    return jnp.concatenate(
        [jnp.concatenate([first, zero], axis=1), jnp.concatenate([lower, last], axis=1)], axis=0
    )


def place_of(box, me):
    return ((box ^ me) & 1) * 4 + (((box >> 1) - (me >> 1)) & 3)


def box_at(place, me):
    return ((((place & 3) + (me >> 1)) & 3) << 1) | ((place >> 2) ^ (me & 1))


def lift_kernel(
    where, basis_in, transfer_in, parent_basis, own_same, own_other, share,
    basis, transfer, rows_of_parents, sems,
):
    me = where[1]
    count = basis.shape[0] // UNROLL

    def copies(group):
        at = pl.ds(group * UNROLL, UNROLL)
        return [
            pltpu.make_async_copy(basis_in.at[at], basis.at[at], sems.at[0, group]),
            pltpu.make_async_copy(transfer_in.at[at], transfer.at[at], sems.at[1, group]),
        ]

    for group in range(count):
        for copy in copies(group):
            copy.start()
    cleared(parent_basis)

    def lift(group):
        for copy in copies(group):
            copy.wait()
        children = [group * UNROLL + step for step in range(UNROLL)]
        terms = inner([transfer[c] for c in children], [basis[c] for c in children])
        for child, term in zip(children, terms):
            parent_basis[where[PARENTS + child]] += term

    each(count, lift)
    diagonals = []
    for parent in range(2):
        lower, both, diagonal = packed(parent_basis[parent])
        rows_of_parents[parent * 256 : parent * 256 + HALF] = lower
        rows_of_parents[parent * 256 + HALF : parent * 256 + 256] = both
        diagonals.append(diagonal)
    for own, first in ((own_same, 0), (own_other, 4)):

        def pack(at):
            box = box_at(first + at, me)
            lower, both, diagonal = packed(basis[box])
            own[at, :HALF] = lower
            own[at, HALF:PART] = both
            own[at, PART:DIAG] = rows_of_parents[pl.ds(pl.multiple_of(box * 64, 64), 64)]
            own[at, DIAG:] = jnp.concatenate(
                [diagonal, *diagonals, jnp.zeros((SHARE - DIAG - 3, HALF), jnp.float32)], axis=0
            )

        each(4, pack)
    share[...] = own_same[0]


def far_kernel(
    where, child_basis, parent_basis, child_blocks, parent_blocks, kept, sent, own, total,
):
    clus, me = where[0], where[1]
    child_groups = child_blocks.shape[0] // UNROLL
    parent_groups = parent_blocks.shape[0] // UNROLL
    cleared(total)
    trash = 4 * PAIR

    def of_children(group):
        rows = [group * UNROLL + step for step in range(UNROLL)]
        nears = [where[CHILD_LIST + 2 * row] for row in rows]
        grams = [child_basis[jnp.where(near >= 0, near - clus * PAIR, 0)] for near in nears]
        for row, term in zip(rows, inner([child_blocks[row] for row in rows], grams)):
            lower, both, diagonal = packed(term)
            far = where[CHILD_LIST + 2 * row + 1]
            slot = place_of(far & 7, me) * 4 + (far >> 3) - clus
            slot = jnp.where(far >= 0, slot, trash)
            total[slot, :HALF] += lower
            total[slot, HALF:PART] += both
            total[slot, DIAG : DIAG + 1] += diagonal

    def of_parents(group):
        rows = [group * UNROLL + step for step in range(UNROLL)]
        nears = [where[PARENT_LIST + 2 * row] for row in rows]
        grams = [parent_basis[jnp.where(near >= 0, near - clus * 2, 0)] for near in nears]
        blocks = [parent_blocks[row] for row in rows]
        for row, term in zip(rows, inner(blocks, grams)):
            lower, both, diagonal = packed(term)
            far = where[PARENT_LIST + 2 * row + 1]
            usable = far >= 0
            offset, parent = (far >> 1) - clus, far & 1
            pieces = (lower[:64], lower[64:], both[:64], both[64:])
            for piece, lines in enumerate(pieces):
                slot = place_of(parent * 4 + piece, me) * 4 + offset
                total[jnp.where(usable, slot, trash), PART:DIAG] += lines
            slot = jnp.where(usable, place_of(0, me) * 4 + offset, trash)
            lines = lax.broadcasted_iota(jnp.int32, (8, HALF), 0)
            total[slot, DIAG:] += jnp.where(lines == parent + 1, diagonal, 0.0)

    each(child_groups, of_children)
    each(parent_groups, of_parents)
    for target, first_place in ((kept, 0), (sent, 4)):

        def hand_out(at):
            place = first_place + at
            own[place] = total[place * 4]
            for offset in range(REACH):
                target[at, offset] = total[place * 4 + 1 + offset]

        each(4, hand_out)


def near_kernel(
    where, after, also_after, child_blocks, parent_blocks, own_terms, own_same, own_other,
    mine, other, *rest,
):
    pieces = rest[:PAIR]
    kept, sent, window, total, rows_of_parents = rest[PAIR:]
    clus, me = where[0], where[1]
    halves = (
        (own_same, 0, 0, 0), (own_other, 0, 4, 0),
        (mine, 0, 0, 1), (other, 0, 4, 1), (mine, 4, 0, 2), (other, 4, 4, 2),
    )
    for source, start, first_place, offset in halves:

        def take_half(at):
            window[first_place + at, offset] = source[start + at]

        each(4, take_half)
    for place, piece in enumerate(pieces):
        window[place, REACH] = piece[...]
    child_groups = child_blocks.shape[0] // UNROLL
    parent_groups = parent_blocks.shape[0] // UNROLL
    cleared(total)
    trash = PAIR + 2

    def of_children(group):
        rows = [group * UNROLL + step for step in range(UNROLL)]
        grams = []
        for row in rows:
            far = where[CHILD_LIST + 2 * row + 1]
            place = place_of(far & 7, me)
            offset = jnp.where(far >= 0, (far >> 3) - clus, 0)
            grams.append(
                halved(
                    window[place, offset, :HALF],
                    window[place, offset, HALF:PART],
                    window[place, offset, DIAG : DIAG + 1],
                )
            )
        for row, term in zip(rows, outer([child_blocks[row] for row in rows], grams)):
            near = where[CHILD_LIST + 2 * row]
            total[jnp.where(near >= 0, near - clus * PAIR, trash)] += term

    def of_parents(group):
        rows = [group * UNROLL + step for step in range(UNROLL)]
        grams = []
        for row in rows:
            far = where[PARENT_LIST + 2 * row + 1]
            parent = far & 1
            offset = jnp.where(far >= 0, (far >> 1) - clus, 0)
            lines = [
                window[place_of(parent * 4 + piece, me), offset, PART:DIAG] for piece in range(4)
            ]
            diagonals = window[0, offset, DIAG:]
            grams.append(
                halved(
                    jnp.concatenate(lines[:2], axis=0),
                    jnp.concatenate(lines[2:], axis=0),
                    jnp.where(parent == 0, diagonals[1:2], diagonals[2:3]),
                )
            )
        blocks = [parent_blocks[row] for row in rows]
        for row, term in zip(rows, outer(blocks, grams)):
            near = where[PARENT_LIST + 2 * row]
            total[jnp.where(near >= 0, PAIR + near - clus * 2, trash)] += term

    each(child_groups, of_children)
    each(parent_groups, of_parents)
    diagonals = []
    for parent in range(2):
        lower, both, diagonal = packed_sum(total[PAIR + parent])
        rows_of_parents[parent * 256 : parent * 256 + HALF] = lower
        rows_of_parents[parent * 256 + HALF : parent * 256 + 256] = both
        diagonals.append(diagonal)
    for target, first_place in ((kept, 0), (sent, 4)):

        def pack(at):
            place = first_place + at
            box = box_at(place, me)
            lower, both, diagonal = packed_sum(total[box])
            target[at, :HALF] = own_terms[place, :HALF] + lower
            target[at, HALF:PART] = own_terms[place, HALF:PART] + both
            target[at, PART:DIAG] = (
                own_terms[place, PART:DIAG]
                + rows_of_parents[pl.ds(pl.multiple_of(box * 64, 64), 64)]
            )
            lines = [jnp.where(box == 0, line, 0.0) for line in diagonals]
            target[at, DIAG:] = own_terms[place, DIAG:] + jnp.concatenate(
                [diagonal, *lines, jnp.zeros((SHARE - DIAG - 3, HALF), jnp.float32)], axis=0
            )

        each(4, pack)


def lower_kernel(where, transfer, upper, *rest):
    pieces, weight, shares, coarse = rest[:PAIR], *rest[PAIR:]
    me = where[1]
    for place in range(PAIR):
        shares[place] = pieces[place][...]
    diagonals = shares[place_of(0, me), DIAG:]
    for parent in range(2):
        rows = [shares[place_of(parent * 4 + piece, me), PART:DIAG] for piece in range(4)]
        coarse[parent] = 0.5 * upper[parent] + halved(
            jnp.concatenate(rows[:2], axis=0),
            jnp.concatenate(rows[2:], axis=0),
            diagonals[parent + 1 : parent + 2],
        )

    def lower(group):
        children = [group * UNROLL + step for step in range(UNROLL)]
        terms = outer(
            [transfer[child] for child in children],
            [coarse[where[PARENTS + child]] for child in children],
        )
        for child, term in zip(children, terms):
            place = place_of(child, me)
            term = term + halved(
                shares[place, :HALF], shares[place, HALF:PART], shares[place, DIAG : DIAG + 1]
            )
            weight[child] = term + term.T

    each(weight.shape[0] // UNROLL, lower)


def call(kernel, name, out_shape, in_specs, out_specs, scratch, products):
    return pl.pallas_call(
        kernel,
        name=name,
        out_shape=out_shape,
        in_specs=in_specs,
        out_specs=out_specs,
        scratch_shapes=scratch,
        compiler_params=pltpu.CompilerParams(vmem_limit_bytes=VMEM_LIMIT),
        cost_estimate=pl.CostEstimate(
            flops=products * 6 * 256**3, bytes_accessed=8 * 2**20, transcendentals=0
        ),
    )


def floats(*shape):
    return jax.ShapeDtypeStruct(shape, jnp.float32)


def to_clus(value, steps):
    count = lax.axis_size("clus")
    return lax.ppermute(value, "clus", [(i, (i + steps) % count) for i in range(count)])


def to_y(value, steps):
    return lax.ppermute(value, "pair", [(i, (i + 2 * steps) % PAIR) for i in range(PAIR)])


def to_core(value):
    return lax.ppermute(value, "pair", [(i, i ^ 1) for i in range(PAIR)])


def everywhere(share):
    pieces = [share] + [to_y(share, -step) for step in range(1, 4)]
    return pieces + [to_core(piece) for piece in pieces]


def per_device(
    child_basis,
    transfer,
    child_parent,
    upper_weight,
    child_pairs,
    child_blocks,
    parent_pairs,
    parent_blocks,
):
    boxes, extent = child_basis.shape[0], child_basis.shape[-1]
    where = jnp.concatenate(
        [
            jnp.stack([lax.axis_index("clus"), lax.axis_index("pair")]).astype(jnp.int32),
            child_parent.reshape(-1),
            child_pairs.reshape(-1),
            parent_pairs.reshape(-1),
        ]
    )

    parent_basis, own_same, own_other, share = call(
        lift_kernel,
        "lift",
        (
            floats(2, extent, extent),
            floats(4, SHARE, HALF),
            floats(4, SHARE, HALF),
            floats(SHARE, HALF),
        ),
        [SMEM, ANY, ANY],
        (VMEM, VMEM, VMEM, VMEM),
        [
            pltpu.VMEM((boxes, extent, extent), jnp.float32),
            pltpu.VMEM((boxes, extent, extent), jnp.float32),
            pltpu.VMEM((512, HALF), jnp.float32),
            pltpu.SemaphoreType.DMA((2, boxes // UNROLL)),
        ],
        16,
    )(where, child_basis, transfer)

    second = to_clus(share, -2)

    kept, sent, own_terms = call(
        far_kernel,
        "far",
        (
            floats(4, REACH, SHARE, HALF),
            floats(4, REACH, SHARE, HALF),
            floats(PAIR, SHARE, HALF),
        ),
        [SMEM, VMEM, VMEM, VMEM, VMEM],
        (VMEM, VMEM, VMEM),
        [
            pltpu.VMEM((4 * PAIR + 1, SHARE, HALF), jnp.float32),
        ],
        40,
    )(where, child_basis, parent_basis, child_blocks, parent_blocks)

    second, own_same, kept, sent = lax.optimization_barrier((second, own_same, kept, sent))
    barrier = lax.optimization_barrier
    chain = to_clus(jnp.concatenate([own_same, second[None]]), -1)
    got = to_core(sent)
    far_first = to_clus(kept[:, 0] + got[:, 0], 1)
    parts = [kept[step, 1:] + got[step, 1:] for step in range(4)]
    received = [
        to_y(jnp.concatenate([parts[step], second[None]]), step) for step in range(1, 4)
    ]
    chain, far_first, received = barrier((chain, far_first, received))

    far_sum = parts[0] + received[0][:2] + received[1][:2] + received[2][:2]
    far_third = to_clus(far_sum[1], 1)
    third = chain[4]
    thirds = [third] + [to_y(third, -step) for step in range(1, 4)]
    mine = jnp.concatenate(
        [chain[:4], second[None], received[2][2:], received[1][2:], received[0][2:]]
    )
    other = to_core(mine)
    far_third, thirds, other, mine = barrier((far_third, thirds, other, mine))

    far_later = to_clus(far_sum[0] + far_third, 2)
    third_pieces = thirds + [to_core(piece) for piece in thirds]

    kept, sent = call(
        near_kernel,
        "near",
        (floats(4, SHARE, HALF), floats(4, SHARE, HALF)),
        [SMEM, ANY, ANY, VMEM, VMEM, VMEM] + [VMEM] * (PAIR + 4),
        (VMEM, VMEM),
        [
            pltpu.VMEM((PAIR, REACH + 1, SHARE, HALF), jnp.float32),
            pltpu.VMEM((PAIR + 3, extent, extent), jnp.float32),
            pltpu.VMEM((512, HALF), jnp.float32),
        ],
        40,
    )(
        where, far_third, far_first, child_blocks, parent_blocks, own_terms, own_same, own_other,
        mine, other, *third_pieces,
    )

    kept, sent, far_later = lax.optimization_barrier((kept, sent, far_later))
    got = to_core(sent)
    parts = [kept[step] + got[step] + far_first[step] for step in range(4)]
    total = parts[0] + far_later
    for step in range(1, 4):
        total = total + to_y(parts[step], step)

    child_weight = call(
        lower_kernel,
        "lower",
        floats(boxes, extent, extent),
        [SMEM, VMEM, VMEM] + [VMEM] * PAIR,
        VMEM,
        [
            pltpu.VMEM((PAIR, SHARE, HALF), jnp.float32),
            pltpu.VMEM((2, extent, extent), jnp.float32),
        ],
        16,
    )(where, transfer, upper_weight, *everywhere(total))
    return child_weight, parent_basis


def solution(mesh):
    return jax.shard_map(
        per_device,
        mesh=mesh,
        in_specs=(
            P("clus", None, None),
            P("clus", None, None),
            P("clus", None),
            P("clus", None, None),
            P(("clus", "pair"), None),
            P(("clus", "pair"), None, None),
            P(("clus", "pair"), None),
            P(("clus", "pair"), None, None),
        ),
        out_specs=(P("clus", None, None), P("clus", None, None)),
        check_vma=False,
    )
```

```python
import functools

import jax
import jax.numpy as jnp
from jax import lax
from jax.experimental import pallas as pl
from jax.experimental.pallas import tpu as pltpu
from jax.sharding import PartitionSpec as P

REACH = 3
PAIR = 8
HALF = 128
PART = 256
DIAG = 320
SHARE = 328
UNROLL = 4
PARENTS = 2
CHILD_LIST = 10
PARENT_LIST = 34
VMEM_LIMIT = 24 * 2**20

NN = (((1,), (0,)), ((), ()))
NT = (((1,), (1,)), ((), ()))
TN = (((0,), (0,)), ((), ()))

VMEM = pl.BlockSpec(memory_space=pltpu.VMEM)
SMEM = pl.BlockSpec(memory_space=pltpu.SMEM)
ANY = pl.BlockSpec(memory_space=pl.ANY)


def split(value):
    high = value.astype(jnp.bfloat16)
    return high, (value - high.astype(jnp.float32)).astype(jnp.bfloat16)


def product(left, right, dims):
    def one(a, b):
        return lax.dot_general(a, b, dims, preferred_element_type=jnp.float32)

    return one(left[0], right[0]) + (one(left[0], right[1]) + one(left[1], right[0]))


def inner(blocks, grams):
    blocks = [split(block) for block in blocks]
    grams = [split(gram) for gram in grams]
    halfway = [split(product(gram, block, NN)) for gram, block in zip(grams, blocks)]
    return [product(block, value, TN) for block, value in zip(blocks, halfway)]


def outer(blocks, grams):
    blocks = [split(block) for block in blocks]
    grams = [split(gram) for gram in grams]
    halfway = [split(product(block, gram, NN)) for gram, block in zip(grams, blocks)]
    return [product(value, block, NT) for block, value in zip(blocks, halfway)]


def each(count, body):
    lax.fori_loop(0, count, lambda i, carry: (body(i), carry)[1], 0)


def cleared(ref):
    def clear(i):
        ref[i] = jnp.zeros(ref.shape[1:], ref.dtype)

    each(ref.shape[0], clear)


def grids():
    rows = lax.broadcasted_iota(jnp.int32, (HALF, HALF), 0)
    cols = lax.broadcasted_iota(jnp.int32, (HALF, HALF), 1)
    return rows, cols


def packed(full):
    rows, cols = grids()
    first, last = full[:HALF, :HALF], full[HALF:, HALF:]
    diagonal = jnp.sum(jnp.where(rows == cols, first, 0.0), axis=0, keepdims=True)
    return full[HALF:, :HALF], jnp.where(rows > cols, first, last), diagonal


def packed_sum(half):
    rows, cols = grids()
    first, last = half[:HALF, :HALF], half[HALF:, HALF:]
    diagonal = jnp.sum(jnp.where(rows == cols, 2.0 * first, 0.0), axis=0, keepdims=True)
    lower = half[HALF:, :HALF] + half[:HALF, HALF:].T
    both = jnp.where(rows > cols, first, last) + jnp.where(rows < cols, first, last).T
    return lower, both, diagonal


def halved(lower, both, diagonal):
    rows, cols = grids()
    zero = jnp.zeros((HALF, HALF), jnp.float32)
    first = jnp.where(rows > cols, both, jnp.where(rows == cols, 0.5 * diagonal, 0.0))
    last = jnp.where(rows < cols, both, jnp.where(rows == cols, 0.5 * both, 0.0))
    return jnp.concatenate(
        [jnp.concatenate([first, zero], axis=1), jnp.concatenate([lower, last], axis=1)], axis=0
    )


def place_of(box, me):
    return ((box ^ me) & 1) * 4 + (((box >> 1) - (me >> 1)) & 3)


def box_at(place, me):
    return ((((place & 3) + (me >> 1)) & 3) << 1) | ((place >> 2) ^ (me & 1))


def lift_kernel(
    where, basis_in, transfer_in, parent_basis, own_same, own_other, share,
    basis, transfer, rows_of_parents, sems,
):
    me = where[1]
    count = basis.shape[0] // UNROLL

    def copies(group):
        at = pl.ds(group * UNROLL, UNROLL)
        return [
            pltpu.make_async_copy(basis_in.at[at], basis.at[at], sems.at[0, group]),
            pltpu.make_async_copy(transfer_in.at[at], transfer.at[at], sems.at[1, group]),
        ]

    for group in range(count):
        for copy in copies(group):
            copy.start()
    cleared(parent_basis)

    def lift(group):
        for copy in copies(group):
            copy.wait()
        children = [group * UNROLL + step for step in range(UNROLL)]
        terms = inner([transfer[c] for c in children], [basis[c] for c in children])
        for child, term in zip(children, terms):
            parent_basis[where[PARENTS + child]] += term

    each(count, lift)
    diagonals = []
    for parent in range(2):
        lower, both, diagonal = packed(parent_basis[parent])
        rows_of_parents[parent * 256 : parent * 256 + HALF] = lower
        rows_of_parents[parent * 256 + HALF : parent * 256 + 256] = both
        diagonals.append(diagonal)
    for own, first in ((own_same, 0), (own_other, 4)):

        def pack(at):
            box = box_at(first + at, me)
            lower, both, diagonal = packed(basis[box])
            own[at, :HALF] = lower
            own[at, HALF:PART] = both
            own[at, PART:DIAG] = rows_of_parents[pl.ds(pl.multiple_of(box * 64, 64), 64)]
            own[at, DIAG:] = jnp.concatenate(
                [diagonal, *diagonals, jnp.zeros((SHARE - DIAG - 3, HALF), jnp.float32)], axis=0
            )

        each(4, pack)
    share[...] = own_same[0]


def far_kernel(
    where, child_basis, parent_basis, child_blocks, parent_blocks, kept, sent, own, total,
):
    clus, me = where[0], where[1]
    child_groups = child_blocks.shape[0] // UNROLL
    parent_groups = parent_blocks.shape[0] // UNROLL
    cleared(total)
    trash = 4 * PAIR

    def of_children(group):
        rows = [group * UNROLL + step for step in range(UNROLL)]
        nears = [where[CHILD_LIST + 2 * row] for row in rows]
        grams = [child_basis[jnp.where(near >= 0, near - clus * PAIR, 0)] for near in nears]
        for row, term in zip(rows, inner([child_blocks[row] for row in rows], grams)):
            lower, both, diagonal = packed(term)
            far = where[CHILD_LIST + 2 * row + 1]
            slot = place_of(far & 7, me) * 4 + (far >> 3) - clus
            slot = jnp.where(far >= 0, slot, trash)
            total[slot, :HALF] += lower
            total[slot, HALF:PART] += both
            total[slot, DIAG : DIAG + 1] += diagonal

    def of_parents(group):
        rows = [group * UNROLL + step for step in range(UNROLL)]
        nears = [where[PARENT_LIST + 2 * row] for row in rows]
        grams = [parent_basis[jnp.where(near >= 0, near - clus * 2, 0)] for near in nears]
        blocks = [parent_blocks[row] for row in rows]
        for row, term in zip(rows, inner(blocks, grams)):
            lower, both, diagonal = packed(term)
            far = where[PARENT_LIST + 2 * row + 1]
            usable = far >= 0
            offset, parent = (far >> 1) - clus, far & 1
            pieces = (lower[:64], lower[64:], both[:64], both[64:])
            for piece, lines in enumerate(pieces):
                slot = place_of(parent * 4 + piece, me) * 4 + offset
                total[jnp.where(usable, slot, trash), PART:DIAG] += lines
            slot = jnp.where(usable, place_of(0, me) * 4 + offset, trash)
            lines = lax.broadcasted_iota(jnp.int32, (8, HALF), 0)
            total[slot, DIAG:] += jnp.where(lines == parent + 1, diagonal, 0.0)

    each(child_groups, of_children)
    each(parent_groups, of_parents)
    for target, first_place in ((kept, 0), (sent, 4)):

        def hand_out(at):
            place = first_place + at
            own[place] = total[place * 4]
            for offset in range(REACH):
                target[at, offset] = total[place * 4 + 1 + offset]

        each(4, hand_out)


def near_kernel(
    where, after, also_after, child_blocks, parent_blocks, own_terms, own_same, own_other,
    mine, other, *rest,
):
    pieces = rest[:PAIR]
    kept, sent, window, total, rows_of_parents = rest[PAIR:]
    clus, me = where[0], where[1]
    halves = (
        (own_same, 0, 0, 0), (own_other, 0, 4, 0),
        (mine, 0, 0, 1), (other, 0, 4, 1), (mine, 4, 0, 2), (other, 4, 4, 2),
    )
    for source, start, first_place, offset in halves:

        def take_half(at):
            window[first_place + at, offset] = source[start + at]

        each(4, take_half)
    for place, piece in enumerate(pieces):
        window[place, REACH] = piece[...]
    child_groups = child_blocks.shape[0] // UNROLL
    parent_groups = parent_blocks.shape[0] // UNROLL
    cleared(total)
    trash = PAIR + 2

    def of_children(group):
        rows = [group * UNROLL + step for step in range(UNROLL)]
        grams = []
        for row in rows:
            far = where[CHILD_LIST + 2 * row + 1]
            place = place_of(far & 7, me)
            offset = jnp.where(far >= 0, (far >> 3) - clus, 0)
            grams.append(
                halved(
                    window[place, offset, :HALF],
                    window[place, offset, HALF:PART],
                    window[place, offset, DIAG : DIAG + 1],
                )
            )
        for row, term in zip(rows, outer([child_blocks[row] for row in rows], grams)):
            near = where[CHILD_LIST + 2 * row]
            total[jnp.where(near >= 0, near - clus * PAIR, trash)] += term

    def of_parents(group):
        rows = [group * UNROLL + step for step in range(UNROLL)]
        grams = []
        for row in rows:
            far = where[PARENT_LIST + 2 * row + 1]
            parent = far & 1
            offset = jnp.where(far >= 0, (far >> 1) - clus, 0)
            lines = [
                window[place_of(parent * 4 + piece, me), offset, PART:DIAG] for piece in range(4)
            ]
            diagonals = window[0, offset, DIAG:]
            grams.append(
                halved(
                    jnp.concatenate(lines[:2], axis=0),
                    jnp.concatenate(lines[2:], axis=0),
                    jnp.where(parent == 0, diagonals[1:2], diagonals[2:3]),
                )
            )
        blocks = [parent_blocks[row] for row in rows]
        for row, term in zip(rows, outer(blocks, grams)):
            near = where[PARENT_LIST + 2 * row]
            total[jnp.where(near >= 0, PAIR + near - clus * 2, trash)] += term

    each(child_groups, of_children)
    each(parent_groups, of_parents)
    diagonals = []
    for parent in range(2):
        lower, both, diagonal = packed_sum(total[PAIR + parent])
        rows_of_parents[parent * 256 : parent * 256 + HALF] = lower
        rows_of_parents[parent * 256 + HALF : parent * 256 + 256] = both
        diagonals.append(diagonal)
    for target, first_place in ((kept, 0), (sent, 4)):

        def pack(at):
            place = first_place + at
            box = box_at(place, me)
            lower, both, diagonal = packed_sum(total[box])
            target[at, :HALF] = own_terms[place, :HALF] + lower
            target[at, HALF:PART] = own_terms[place, HALF:PART] + both
            target[at, PART:DIAG] = (
                own_terms[place, PART:DIAG]
                + rows_of_parents[pl.ds(pl.multiple_of(box * 64, 64), 64)]
            )
            lines = [jnp.where(box == 0, line, 0.0) for line in diagonals]
            target[at, DIAG:] = own_terms[place, DIAG:] + jnp.concatenate(
                [diagonal, *lines, jnp.zeros((SHARE - DIAG - 3, HALF), jnp.float32)], axis=0
            )

        each(4, pack)


def lower_kernel(where, transfer, upper, *rest):
    pieces, weight, shares, coarse = rest[:PAIR], *rest[PAIR:]
    me = where[1]
    for place in range(PAIR):
        shares[place] = pieces[place][...]
    diagonals = shares[place_of(0, me), DIAG:]
    for parent in range(2):
        rows = [shares[place_of(parent * 4 + piece, me), PART:DIAG] for piece in range(4)]
        coarse[parent] = 0.5 * upper[parent] + halved(
            jnp.concatenate(rows[:2], axis=0),
            jnp.concatenate(rows[2:], axis=0),
            diagonals[parent + 1 : parent + 2],
        )

    def lower(group):
        children = [group * UNROLL + step for step in range(UNROLL)]
        terms = outer(
            [transfer[child] for child in children],
            [coarse[where[PARENTS + child]] for child in children],
        )
        for child, term in zip(children, terms):
            place = place_of(child, me)
            term = term + halved(
                shares[place, :HALF], shares[place, HALF:PART], shares[place, DIAG : DIAG + 1]
            )
            weight[child] = term + term.T

    each(weight.shape[0] // UNROLL, lower)


def call(kernel, name, out_shape, in_specs, out_specs, scratch, products):
    return pl.pallas_call(
        kernel,
        name=name,
        out_shape=out_shape,
        in_specs=in_specs,
        out_specs=out_specs,
        scratch_shapes=scratch,
        compiler_params=pltpu.CompilerParams(vmem_limit_bytes=VMEM_LIMIT),
        cost_estimate=pl.CostEstimate(
            flops=products * 6 * 256**3, bytes_accessed=8 * 2**20, transcendentals=0
        ),
    )


def floats(*shape):
    return jax.ShapeDtypeStruct(shape, jnp.float32)


def to_clus(value, steps):
    count = lax.axis_size("clus")
    return lax.ppermute(value, "clus", [(i, (i + steps) % count) for i in range(count)])


def to_y(value, steps):
    return lax.ppermute(value, "pair", [(i, (i + 2 * steps) % PAIR) for i in range(PAIR)])


def to_core(value):
    return lax.ppermute(value, "pair", [(i, i ^ 1) for i in range(PAIR)])


def everywhere(share):
    pieces = [share] + [to_y(share, -step) for step in range(1, 4)]
    return pieces + [to_core(piece) for piece in pieces]


def per_device(
    child_basis,
    transfer,
    child_parent,
    upper_weight,
    child_pairs,
    child_blocks,
    parent_pairs,
    parent_blocks,
):
    boxes, extent = child_basis.shape[0], child_basis.shape[-1]
    early = jnp.concatenate(
        [
            jnp.stack([lax.axis_index("clus"), lax.axis_index("pair")]).astype(jnp.int32),
            child_parent.reshape(-1),
        ]
    )

    parent_basis, own_same, own_other, share = call(
        lift_kernel,
        "lift",
        (
            floats(2, extent, extent),
            floats(4, SHARE, HALF),
            floats(4, SHARE, HALF),
            floats(SHARE, HALF),
        ),
        [SMEM, ANY, ANY],
        (VMEM, VMEM, VMEM, VMEM),
        [
            pltpu.VMEM((boxes, extent, extent), jnp.float32),
            pltpu.VMEM((boxes, extent, extent), jnp.float32),
            pltpu.VMEM((512, HALF), jnp.float32),
            pltpu.SemaphoreType.DMA((2, boxes // UNROLL)),
        ],
        16,
    )(early, child_basis, transfer)

    share, child_pairs, parent_pairs = lax.optimization_barrier((share, child_pairs, parent_pairs))
    where = jnp.concatenate([early, child_pairs.reshape(-1), parent_pairs.reshape(-1)])

    second = to_clus(share, -2)

    kept, sent, own_terms = call(
        far_kernel,
        "far",
        (
            floats(4, REACH, SHARE, HALF),
            floats(4, REACH, SHARE, HALF),
            floats(PAIR, SHARE, HALF),
        ),
        [SMEM, VMEM, VMEM, VMEM, VMEM],
        (VMEM, VMEM, VMEM),
        [
            pltpu.VMEM((4 * PAIR + 1, SHARE, HALF), jnp.float32),
        ],
        40,
    )(where, child_basis, parent_basis, child_blocks, parent_blocks)

    second, own_same, kept, sent = lax.optimization_barrier((second, own_same, kept, sent))
    barrier = lax.optimization_barrier
    chain = to_clus(jnp.concatenate([own_same, second[None]]), -1)
    got = to_core(sent)
    far_first = to_clus(kept[:, 0] + got[:, 0], 1)
    parts = [kept[step, 1:] + got[step, 1:] for step in range(4)]
    received = [
        to_y(jnp.concatenate([parts[step], second[None]]), step) for step in range(1, 4)
    ]
    chain, far_first, received = barrier((chain, far_first, received))

    far_sum = parts[0] + received[0][:2] + received[1][:2] + received[2][:2]
    far_third = to_clus(far_sum[1], 1)
    third = chain[4]
    thirds = [third] + [to_y(third, -step) for step in range(1, 4)]
    mine = jnp.concatenate(
        [chain[:4], second[None], received[2][2:], received[1][2:], received[0][2:]]
    )
    other = to_core(mine)
    far_third, thirds, other, mine = barrier((far_third, thirds, other, mine))

    far_later = to_clus(far_sum[0] + far_third, 2)
    third_pieces = thirds + [to_core(piece) for piece in thirds]

    kept, sent = call(
        near_kernel,
        "near",
        (floats(4, SHARE, HALF), floats(4, SHARE, HALF)),
        [SMEM, ANY, ANY, VMEM, VMEM, VMEM] + [VMEM] * (PAIR + 4),
        (VMEM, VMEM),
        [
            pltpu.VMEM((PAIR, REACH + 1, SHARE, HALF), jnp.float32),
            pltpu.VMEM((PAIR + 3, extent, extent), jnp.float32),
            pltpu.VMEM((512, HALF), jnp.float32),
        ],
        40,
    )(
        where, far_third, far_first, child_blocks, parent_blocks, own_terms, own_same, own_other,
        mine, other, *third_pieces,
    )

    kept, sent, far_later = lax.optimization_barrier((kept, sent, far_later))
    got = to_core(sent)
    parts = [kept[step] + got[step] + far_first[step] for step in range(4)]
    total = parts[0] + far_later
    for step in range(1, 4):
        total = total + to_y(parts[step], step)

    child_weight = call(
        lower_kernel,
        "lower",
        floats(boxes, extent, extent),
        [SMEM, VMEM, VMEM] + [VMEM] * PAIR,
        VMEM,
        [
            pltpu.VMEM((PAIR, SHARE, HALF), jnp.float32),
            pltpu.VMEM((2, extent, extent), jnp.float32),
        ],
        16,
    )(where, transfer, upper_weight, *everywhere(total))
    return child_weight, parent_basis


def solution(mesh):
    return jax.shard_map(
        per_device,
        mesh=mesh,
        in_specs=(
            P("clus", None, None),
            P("clus", None, None),
            P("clus", None),
            P("clus", None, None),
            P(("clus", "pair"), None),
            P(("clus", "pair"), None, None),
            P(("clus", "pair"), None),
            P(("clus", "pair"), None, None),
        ),
        out_specs=(P("clus", None, None), P("clus", None, None)),
        check_vma=False,
    )
```
